32 devices in a mesh: section: 8 (over y, x, core), tensor: 4 (over z).
Axes of the slice: x: 2, y: 2, z: 4, core: 2. Of those that a mesh axis runs over, the one named last changes fastest.
Arguments:
- inputs: bfloat16 [4, 128, 16384], P(None, None, 'tensor'), may hold values from -6 to 6
- state: float32 [8, 128, 16, 16384], P('section', None, None, 'tensor'), may hold values from -4 to 4
- pool: float32 [8, 3, 16, 16384], P('section', None, None, 'tensor'), may hold values from -4 to 4
- x_weight: bfloat16 [8, 16384, 544], P('section', 'tensor'), may hold values from -0.046875 to 0.046875
- dt_weight: bfloat16 [8, 512, 16384], P('section', None, 'tensor'), may hold values from -0.25 to 0.25
- dt_bias: float32 [8, 16384], P('section', 'tensor'), may hold values from -4 to -1
- a_log: float32 [8, 16, 16384], P('section', None, 'tensor'), may hold values from 0 to 2.8
- skip: float32 [8, 16384], P('section', 'tensor'), may hold values from 0.5 to 1.5
- gain: float32 [8, 16384], P('section', 'tensor'), may hold values from 0.1 to 1.9
- gate_input: bfloat16 [8, 4, 128, 16384], P('section', None, None, 'tensor'), may hold values from -6 to 6
- swap_plan: int32 [3, 8, 3], replicated, may hold values from 0 to 127, as said below
- evict_plan: int32 [3, 8, 3], replicated, may hold values from 0 to 127, as said below
Outputs:
- mixer_out: bfloat16 [8, 4, 128, 16384], P('section', None, None, 'tensor')
- final_state: float32 [8, 128, 16, 16384], P('section', None, None, 'tensor')
- pool_out: float32 [8, 3, 16, 16384], P('section', None, None, 'tensor')
The draws below stay inside these ranges and needn't reach their ends.
Inputs may be any that keep to these rules, and one draw needn't show every extreme that they name: `swap_plan`: row 0 names requests below 128, row 1 holders along section below 8, row 2 slots below 3. Within one layer the 3 requests are distinct and the 3 holders are distinct. `evict_plan`: row 0 names requests below 128, row 1 holders along section below 8, row 2 slots below 3. Within one layer the 3 requests are distinct and the 3 holders are distinct; no pair of holder and slot is named twice in the whole plan.
All inputs are finite; a program needn't handle non-finite values.
Results may differ from the reference program's by a relative error of at most 0.035.
Values may be sent and summed in bfloat16 or wider, within the bound.
No kernel may reach another device: no remote copies, remote signals or barrier semaphores. Data moves between devices by JAX's collectives and lax.ppermute only.
A program may use at most 192 MiB of HBM per device.

```python
import jax
import jax.numpy as jnp
from jax import lax

D_INNER = 16384
STATE = 16
DT_RANK = 512
STEPS = 4
REQ = 128
LAYERS = 8
HOLDERS = 8
SWAP = 3
SLOTS = 3


def distinct_requests(key):
    scores = jax.random.randint(key, (LAYERS, REQ), 0, 1048576) * REQ + jnp.arange(REQ, dtype=jnp.int32)[None, :]
    order = jnp.argsort(scores, axis=1, stable=True).astype(jnp.int32)
    chosen = order[:, :SWAP]
    return ((chosen + (REQ - 1) - chosen[:, 0:1]) % REQ).astype(jnp.int32)


def draw_swap_plan(key, part):
    key = jax.random.fold_in(key, 11)
    first, second, third = jax.random.split(key, 3)
    requests = distinct_requests(first)
    half = HOLDERS // 2
    others = jax.random.permutation(second, HOLDERS - 1)[:SWAP - 1].astype(jnp.int32)
    others = others + (others >= half).astype(jnp.int32)
    offsets = jnp.concatenate([jnp.full((1,), half, jnp.int32), others]).astype(jnp.int32)
    holders = (jnp.arange(LAYERS, dtype=jnp.int32)[:, None] + offsets[None, :]) % HOLDERS
    slots = jax.random.randint(third, (LAYERS, SWAP), 0, SLOTS).astype(jnp.int32)
    return jnp.stack([requests, holders, slots])


def draw_evict_plan(key, part):
    key = jax.random.fold_in(key, 23)
    first, second, third = jax.random.split(key, 3)
    requests = distinct_requests(first)
    offsets = jax.random.permutation(second, HOLDERS)[:SWAP].astype(jnp.int32)
    holders = (jnp.arange(LAYERS, dtype=jnp.int32)[:, None] + offsets[None, :]) % HOLDERS
    rotation = jax.random.randint(third, (), 0, SLOTS).astype(jnp.int32)
    column = (jnp.arange(SWAP, dtype=jnp.int32) + rotation) % SLOTS
    slots = jnp.broadcast_to(column[None, :], (LAYERS, SWAP)).astype(jnp.int32)
    return jnp.stack([requests, holders, slots])


def level_of(rng, shape, shards, smallest, high):
    loudness, own = 1.0, jax.random.fold_in(rng, 6)
    for dim, parts in shards:
        steps = jnp.exp(jax.random.uniform(jax.random.fold_in(own, dim), (parts,), jnp.float32, smallest / len(shards), high / len(shards)))
        loudness = loudness * jnp.repeat(steps, shape[dim] // parts).reshape([-1 if axis == dim else 1 for axis in range(len(shape))])
    return loudness


def bell_draw(own_key, shape, spread, limit, cuts=(), kind=jnp.bfloat16):
    drawn = spread * jax.random.normal(own_key, shape, jnp.float32)
    if cuts:
        drawn = drawn * level_of(own_key, shape, cuts, -0.22, 0.18)
    return jnp.clip(drawn, -limit, limit).astype(kind)


def setup_inputs(seed: int = 0) -> dict:
    streams_of = jax.random.split(jax.random.key(seed), 13)
    inputs = bell_draw(streams_of[0], (STEPS, REQ, D_INNER), 1.0, 6.0, ((2, 4),))
    state = bell_draw(streams_of[1], (LAYERS, REQ, STATE, D_INNER), 0.5, 4.0, ((0, 8), (3, 4)), jnp.float32)
    pool = bell_draw(streams_of[2], (HOLDERS, SLOTS, STATE, D_INNER), 0.5, 4.0, ((0, 8), (3, 4)), jnp.float32)
    x_weight = bell_draw(streams_of[3], (LAYERS, D_INNER, DT_RANK + 2 * STATE), D_INNER ** -0.5, 0.046875, ((0, 8), (1, 4)))
    dt_weight = bell_draw(streams_of[4], (LAYERS, DT_RANK, D_INNER), DT_RANK ** -0.5, 0.25, ((0, 8), (2, 4)))
    dt_bias = jnp.clip(-4.0 + 3.0 * jax.random.uniform(streams_of[5], (LAYERS, D_INNER), jnp.float32) ** level_of(streams_of[5], (LAYERS, D_INNER), ((0, 8), (1, 4)), -0.2, 0.2), -4.0, -1.0)
    a_log = jnp.clip(2.8 * jax.random.uniform(streams_of[6], (LAYERS, STATE, D_INNER), jnp.float32) ** level_of(streams_of[6], (LAYERS, STATE, D_INNER), ((0, 8), (2, 4)), -0.2, 0.2), 0.0, 2.8)
    skip = jnp.clip(0.5 + 1.0 * jax.random.uniform(streams_of[7], (LAYERS, D_INNER), jnp.float32) ** level_of(streams_of[7], (LAYERS, D_INNER), ((0, 8), (1, 4)), -0.2, 0.2), 0.5, 1.5)
    gain = jnp.clip(1.0 + 0.18 * jax.random.normal(streams_of[8], (LAYERS, D_INNER), jnp.float32), 0.1, 1.9)
    gate_input = bell_draw(streams_of[9], (LAYERS, STEPS, REQ, D_INNER), 1.0, 6.0, ((0, 8), (3, 4)))
    swap_plan = draw_swap_plan(jax.random.fold_in(streams_of[12], 71), 0)
    evict_plan = draw_evict_plan(jax.random.fold_in(streams_of[12], 71), 0)
    return dict(inputs=inputs, state=state, pool=pool, x_weight=x_weight, dt_weight=dt_weight, dt_bias=dt_bias, a_log=a_log, skip=skip, gain=gain, gate_input=gate_input, swap_plan=swap_plan, evict_plan=evict_plan)


def reference(inputs, state, pool, x_weight, dt_weight, dt_bias, a_log, skip, gain, gate_input, swap_plan, evict_plan):
    stream = inputs
    pool_out = pool
    mixed_all = []
    finals = []
    for layer in range(LAYERS):
        hold = state[layer]
        hold = hold.at[swap_plan[0, layer]].set(pool[swap_plan[1, layer], swap_plan[2, layer]])
        outs = []
        for step in range(STEPS):
            widened = stream[step].astype(jnp.float32)
            meansq = lax.optimization_barrier(jnp.sum(widened * widened, axis=1, keepdims=True)) / D_INNER
            root = jnp.sqrt(meansq + 1e-05)
            scaled = (widened * gain[layer]).astype(jnp.bfloat16)
            proj = jnp.dot(scaled, x_weight[layer], preferred_element_type=jnp.float32) / root
            low = proj[:, :DT_RANK].astype(jnp.bfloat16)
            step_size = jax.nn.softplus(jnp.dot(low, dt_weight[layer], preferred_element_type=jnp.float32) + dt_bias[layer])
            normed_f = scaled.astype(jnp.float32) / root
            decay = jnp.exp(-step_size[:, None, :] * jnp.exp(a_log[layer])[None])
            hold = decay * hold + (step_size * normed_f)[:, None, :] * proj[:, DT_RANK:DT_RANK + STATE, None]
            mixed = lax.optimization_barrier(jnp.sum(hold * proj[:, DT_RANK + STATE:, None], axis=1)) + skip[layer] * normed_f
            outs.append((mixed * jax.nn.silu(gate_input[layer, step].astype(jnp.float32))).astype(jnp.bfloat16))
        layer_out = jnp.stack(outs)
        mixed_all.append(layer_out)
        stream = (stream.astype(jnp.float32) + layer_out.astype(jnp.float32)).astype(jnp.bfloat16)
        finals.append(hold)
        pool_out = pool_out.at[evict_plan[1, layer], evict_plan[2, layer]].set(hold[evict_plan[0, layer]])
    return (jnp.stack(mixed_all), jnp.stack(finals), pool_out)
```

```python
import functools

import jax
import jax.numpy as jnp
from jax import lax
from jax.experimental import pallas as pl
from jax.experimental.pallas import tpu as pltpu
from jax.sharding import PartitionSpec as P

ROWS = 16
LANES = 128
COLS = 512
DEPTH = 1024
ANY = pl.BlockSpec(memory_space=pl.ANY)
VMEM = pl.BlockSpec(memory_space=pltpu.VMEM)
SMEM = pl.BlockSpec(memory_space=pltpu.SMEM)
LOG2E = 1.4426950408889634


def project_kernel(meta, arrived, inputs, gain, weight, out, stream, held, stream_sem, weight_sem):
    steps, rows, channels = stream.shape
    rank = out.shape[2] - LANES
    extra = weight.shape[1] - rank
    depth = min(DEPTH, channels)
    parts = channels // depth

    @pl.when(meta[1] == 1)
    def _():
        first = pl.multiple_of(meta[0], ROWS)
        fetch = [
            pltpu.make_async_copy(
                weight.at[0, :, pl.ds(k * depth, depth)],
                held.at[:, pl.ds(k * depth, depth)],
                weight_sem.at[k],
            )
            for k in range(parts)
        ]

        @pl.when(meta[2] == 0)
        def _():
            pltpu.make_async_copy(inputs.at[:, pl.ds(first, rows)], stream, stream_sem).start()

        @pl.when(meta[2] > 0)
        def _():
            pltpu.make_async_copy(arrived, stream, stream_sem).start()

        for copy in fetch:
            copy.start()
        pltpu.make_async_copy(arrived, stream, stream_sem).wait()
        total = jnp.zeros((steps * rows, rank + extra), jnp.float32)
        squares = jnp.zeros((steps * rows, 1), jnp.float32)
        for k in range(parts):
            part = pl.ds(k * depth, depth)
            wide = stream[:, :, part].astype(jnp.float32).reshape(steps * rows, depth)
            squares += jnp.sum(wide * wide, axis=1, keepdims=True)
            scaled = (wide * gain[:, part]).astype(jnp.bfloat16)
            fetch[k].wait()
            total += lax.dot_general(
                scaled,
                held[:, part],
                (((1,), (1,)), ((), ())),
                preferred_element_type=jnp.float32,
            )
        lane = lax.broadcasted_iota(jnp.int32, (steps * rows, LANES), 1)
        high = squares.astype(jnp.bfloat16).astype(jnp.float32)
        low = total[:, :rank].astype(jnp.bfloat16)
        tail = jnp.concatenate(
            [total[:, rank:], jnp.zeros((steps * rows, LANES - extra), jnp.float32)], axis=1
        )
        tail = jnp.where(lane == extra, high, jnp.where(lane == extra + 1, squares - high, tail))
        tail = tail.astype(jnp.bfloat16)
        for copy in range(out.shape[0]):
            out[copy, :, :rank] = low
            out[copy, :, rank:] = tail


def softplus(value):
    small = jnp.exp(-jnp.abs(value))
    return jnp.maximum(value, 0.0) + jnp.where(
        small < 1e-3, small - 0.5 * small * small, jnp.log(1.0 + small)
    )


def mix_kernel(
    width,
    layers,
    meta,
    plan,
    summands,
    arrived,
    inputs,
    state,
    landed,
    dt_weight,
    dt_bias,
    rates,
    skip,
    gain,
    gate,
    final_in,
    mixed_in,
    leaving_in,
    onward,
    final,
    mixed,
    leaving,
    stream,
    gates,
    result,
    hold,
    held,
    going,
    sizes,
    drives,
    totals,
    spread,
    sems,
    state_sem,
    weight_sem,
    final_sem,
    mixed_sem,
    going_sem,
):
    steps, rows, channels = stream.shape
    units = steps * rows
    rank = held.shape[0]
    states = rates.shape[0]
    swaps = going.shape[0]
    cols = min(COLS, channels)
    parts = channels // cols
    strips = cols // LANES
    flat = hold.reshape(channels // LANES * rows * states, LANES)

    @pl.when(meta[1] == 1)
    def _():
        first = pl.multiple_of(meta[0], ROWS)
        layer = meta[2]

        def planned(which, row, k):
            return plan[((which * 3 + row) * layers + layer) * swaps + k]

        @pl.when(layer == 0)
        def _():
            pltpu.make_async_copy(inputs.at[:, pl.ds(first, rows)], stream, sems.at[0]).start()

        @pl.when(layer > 0)
        def _():
            pltpu.make_async_copy(arrived, stream, sems.at[0]).start()

        gate_copy = pltpu.make_async_copy(gate.at[0, :, pl.ds(first, rows)], gates, sems.at[1])

        def at(j):
            return pl.ds(pl.multiple_of(j * cols, cols), cols)

        def weight_copy(j):
            return pltpu.make_async_copy(
                dt_weight.at[0, :, at(j)], held.at[:, at(j)], weight_sem.at[j]
            )

        def strip_at(c):
            return pl.ds(pl.multiple_of(c * LANES, LANES), LANES)

        def state_copy(c):
            return pltpu.make_async_copy(
                state.at[0, pl.ds(first, rows), :, strip_at(c)], hold.at[c], state_sem.at[c]
            )

        def final_copy(c):
            return pltpu.make_async_copy(
                hold.at[c], final.at[0, pl.ds(first, rows), :, strip_at(c)], final_sem.at[c]
            )

        def mixed_copy(j):
            return pltpu.make_async_copy(
                result.at[:, :, at(j)], mixed.at[0, :, pl.ds(first, rows), at(j)], mixed_sem.at[j]
            )

        def going_copy(k):
            return pltpu.make_async_copy(
                going.at[k], leaving.at[planned(1, 1, k)], going_sem.at[k]
            )

        for j in range(parts):
            weight_copy(j).start()
            for c in range(strips):
                state_copy(j * strips + c).start()
            if j == 0:
                gate_copy.start()

        total = jnp.sum(summands[...].astype(jnp.float32), axis=0)
        tail = total[:, rank:]
        squares = tail[:, 2 * states : 2 * states + 1] + tail[:, 2 * states + 1 : 2 * states + 2]
        inverse = 1.0 / jnp.sqrt(squares / width + 1e-05)
        low = (total[:, :rank] * inverse).astype(jnp.bfloat16)
        tail = tail * inverse
        for t in range(steps):
            for k in range(2 * states):
                column = tail[t * rows : (t + 1) * rows, k : k + 1]
                spread[t, k] = jnp.broadcast_to(column, (rows, LANES)).astype(jnp.bfloat16)
        pltpu.make_async_copy(arrived, stream, sems.at[0]).wait()
        gate_copy.wait()

        def part(j, carry):
            here = at(j)
            weight_copy(j).wait()
            size = softplus(
                jnp.dot(low, held[:, here], preferred_element_type=jnp.float32) + dt_bias[:, here]
            )
            wide = stream[:, :, here].astype(jnp.float32).reshape(units, cols)
            scaled = (wide * gain[:, here]).astype(jnp.bfloat16).astype(jnp.float32)
            normed = scaled * inverse
            sizes[...] = size.astype(jnp.bfloat16).reshape(steps, rows, cols)
            drives[...] = (size * normed).astype(jnp.bfloat16).reshape(steps, rows, cols)
            for c in range(strips):
                state_copy(j * strips + c).wait()
            for k in range(swaps):
                place = planned(0, 0, k) - first

                @pl.when((place >= 0) & (place < rows))
                def _():
                    for c in range(strips):
                        g = j * strips + c
                        hold[g, place] = landed[planned(0, 1, k), :, strip_at(g)].astype(
                            jnp.float32
                        )

            def strip(c, carry):
                inside = strip_at(c)
                lanes = strip_at(j * strips + c)
                base = (j * strips + c) * rows * states
                size = [sizes[t, :, inside] for t in range(steps)]
                drive = [drives[t, :, inside] for t in range(steps)]
                summed = [None] * steps
                group = [None] * steps
                for n in range(states):
                    rate = rates[n, :, lanes]
                    row = pl.ds(base + n, rows, stride=states)
                    h = flat[row, :].astype(jnp.bfloat16)
                    for t in range(steps):
                        h = jnp.exp2(size[t] * rate) * h + drive[t] * spread[t, n]
                        term = h * spread[t, states + n]
                        group[t] = term if n % 4 == 0 else group[t] + term
                        if n % 4 == 3:
                            term = group[t].astype(jnp.float32)
                            summed[t] = term if summed[t] is None else summed[t] + term
                    flat[row, :] = h.astype(jnp.float32)
                for t in range(steps):
                    totals[t * rows : (t + 1) * rows, inside] = summed[t]
                return carry

            lax.fori_loop(0, strips, strip, 0)
            for c in range(strips):
                final_copy(j * strips + c).start()
            for k in range(swaps):
                place = planned(1, 0, k) - first

                @pl.when((place >= 0) & (place < rows))
                def _():
                    for c in range(strips):
                        g = j * strips + c
                        going[k, :, strip_at(g)] = hold[g, place].astype(jnp.bfloat16)

            opened = gates[:, :, here].astype(jnp.float32).reshape(units, cols)
            value = (totals[...] + skip[:, here] * normed) * (opened * jax.nn.sigmoid(opened))
            value = value.astype(jnp.bfloat16)
            result[:, :, here] = value.reshape(steps, rows, cols)
            passed = (wide + value.astype(jnp.float32)).astype(jnp.bfloat16)
            onward[:, :, here] = passed.reshape(steps, rows, cols)
            mixed_copy(j).start()
            return carry

        lax.fori_loop(0, parts, part, 0)
        for k in range(swaps):
            place = planned(1, 0, k) - first

            @pl.when((place >= 0) & (place < rows))
            def _():
                going_copy(k).start()
                going_copy(k).wait()

        for j in range(parts):
            mixed_copy(j).wait()
        for c in range(parts * strips):
            final_copy(c).wait()


def pick_kernel(meta, plan, store, out):
    layers = out.shape[0]
    swaps = plan.shape[0] // (6 * layers)
    for layer in range(layers):
        slot = 0
        for k in range(swaps):
            asked = plan[(layers + layer) * swaps + k] == meta[0]
            slot = jnp.where(asked, plan[(2 * layers + layer) * swaps + k], slot)
        out[layer] = store[0, slot].astype(out.dtype)


def keep_kernel(meta, plan, store, returned, out):
    layers = returned.shape[0]
    swaps = plan.shape[0] // (6 * layers)
    for slot in range(store.shape[1]):
        source = -1
        for layer in range(layers):
            for k in range(swaps):
                named = (plan[(4 * layers + layer) * swaps + k] == meta[0]) & (
                    plan[(5 * layers + layer) * swaps + k] == slot
                )
                source = jnp.where(named, layer, source)

        @pl.when(source >= 0)
        def _():
            out[0, slot] = returned[source].astype(out.dtype)

        @pl.when(source < 0)
        def _():
            out[0, slot] = store[0, slot]


def leave(*refs):
    pass


def empty(shapes):
    return pl.pallas_call(leave, out_shape=shapes, out_specs=[ANY] * len(shapes))()


def shards(
    inputs,
    state,
    pool,
    x_weight,
    dt_weight,
    dt_bias,
    a_log,
    skip,
    gain,
    gate_input,
    swap_plan,
    evict_plan,
):
    section = lax.axis_index("section")
    holders = lax.axis_size("section")
    peers = lax.axis_size("tensor")
    channels = x_weight.shape[1]
    width = channels * peers
    rank = dt_weight.shape[1]
    states = a_log.shape[1]
    requests = state.shape[1]
    steps = inputs.shape[0]
    swaps = swap_plan.shape[2]
    units = requests // ROWS
    turns = units + holders - 1
    plan = jnp.concatenate([swap_plan.reshape(-1), evict_plan.reshape(-1)])
    weight = jnp.swapaxes(x_weight, 1, 2)
    rates = jnp.broadcast_to(
        (-LOG2E * jnp.exp(a_log[0])).astype(jnp.bfloat16)[:, None], (states, ROWS, channels)
    )
    place = section.astype(jnp.int32)[None]
    route = [(i, i + 1) for i in range(holders - 1)]

    stream_shape = jax.ShapeDtypeStruct((steps, ROWS, channels), jnp.bfloat16)
    partial_shape = jax.ShapeDtypeStruct((peers, steps * ROWS, rank + LANES), jnp.bfloat16)
    state_shape = jax.ShapeDtypeStruct(state.shape, state.dtype)
    mixed_shape = jax.ShapeDtypeStruct(gate_input.shape, gate_input.dtype)
    moved_shape = jax.ShapeDtypeStruct((holders, states, channels), jnp.bfloat16)

    def meta_of(turn):
        unit = turn - section
        valid = (unit >= 0) & (unit < units)
        first = jnp.clip(unit, 0, units - 1) * ROWS
        return jnp.stack([first, valid, section]).astype(jnp.int32)

    def project(meta, arrived):
        depth = min(DEPTH, channels)
        return pl.pallas_call(
            project_kernel,
            out_shape=partial_shape,
            in_specs=[SMEM, ANY, ANY, VMEM, ANY],
            out_specs=VMEM,
            scratch_shapes=[
                pltpu.VMEM(stream_shape.shape, jnp.bfloat16),
                pltpu.VMEM(weight.shape[1:], jnp.bfloat16),
                pltpu.SemaphoreType.DMA,
                pltpu.SemaphoreType.DMA((channels // depth,)),
            ],
            compiler_params=pltpu.CompilerParams(vmem_limit_bytes=24 * 2**20),
            cost_estimate=pl.CostEstimate(
                flops=2 * steps * ROWS * channels * (rank + LANES),
                bytes_accessed=2 * channels * (rank + LANES),
                transcendentals=0,
            ),
            name="project",
        )(meta, arrived, inputs, gain, weight)

    def mix(meta, summands, arrived, final, mixed, leaving):
        cols = min(COLS, channels)
        parts = channels // cols
        rows = steps * ROWS
        return pl.pallas_call(
            functools.partial(mix_kernel, width, holders),
            out_shape=[stream_shape, state_shape, mixed_shape, moved_shape],
            in_specs=[SMEM, SMEM, VMEM, ANY, ANY, ANY, VMEM, ANY, VMEM, VMEM, VMEM, VMEM]
            + [ANY] * 4,
            out_specs=[VMEM, ANY, ANY, ANY],
            scratch_shapes=[
                pltpu.VMEM(stream_shape.shape, jnp.bfloat16),
                pltpu.VMEM(stream_shape.shape, jnp.bfloat16),
                pltpu.VMEM(stream_shape.shape, jnp.bfloat16),
                pltpu.VMEM((channels // LANES, ROWS, states, LANES), jnp.float32),
                pltpu.VMEM((rank, channels), jnp.bfloat16),
                pltpu.VMEM((swaps, states, channels), jnp.bfloat16),
                pltpu.VMEM((steps, ROWS, cols), jnp.bfloat16),
                pltpu.VMEM((steps, ROWS, cols), jnp.bfloat16),
                pltpu.VMEM((rows, cols), jnp.float32),
                pltpu.VMEM((steps, 2 * states, ROWS, LANES), jnp.bfloat16),
                pltpu.SemaphoreType.DMA((2,)),
                pltpu.SemaphoreType.DMA((channels // LANES,)),
                pltpu.SemaphoreType.DMA((parts,)),
                pltpu.SemaphoreType.DMA((channels // LANES,)),
                pltpu.SemaphoreType.DMA((parts,)),
                pltpu.SemaphoreType.DMA((swaps,)),
            ],
            input_output_aliases={13: 1, 14: 2, 15: 3},
            compiler_params=pltpu.CompilerParams(vmem_limit_bytes=24 * 2**20),
            cost_estimate=pl.CostEstimate(
                flops=2 * rows * channels * rank + 8 * rows * states * channels,
                bytes_accessed=2 * channels * rank + 8 * ROWS * states * channels,
                transcendentals=rows * states * channels,
            ),
            name="mix",
        )(
            meta,
            plan,
            summands,
            arrived,
            inputs,
            state,
            landed,
            dt_weight,
            dt_bias,
            rates,
            skip,
            gain,
            gate_input,
            final,
            mixed,
            leaving,
        )

    def exchange(partial):
        return lax.all_to_all(partial, "tensor", split_axis=0, concat_axis=0, tiled=True)

    def swap(block):
        return lax.all_to_all(block, "section", split_axis=0, concat_axis=0, tiled=True)

    def turn(index, carry):
        summands, stream, *kept = carry
        sent, *kept = mix(meta_of(index), summands, stream, *kept)
        stream = lax.ppermute(sent, "section", route)
        summands = exchange(project(meta_of(index + 1), stream))
        return summands, stream, *kept

    picked = pl.pallas_call(
        pick_kernel, out_shape=moved_shape, in_specs=[SMEM, SMEM, VMEM], out_specs=VMEM, name="pick"
    )(place, plan, pool)
    landed = swap(picked)
    kept = empty([state_shape, mixed_shape, moved_shape])
    stream = jnp.zeros(stream_shape.shape, jnp.bfloat16)
    summands = exchange(project(meta_of(0), stream))
    summands, stream, *kept = lax.fori_loop(0, turns - 1, turn, (summands, stream, *kept))
    _, final, mixed, leaving = mix(meta_of(turns - 1), summands, stream, *kept)
    stored = pl.pallas_call(
        keep_kernel,
        out_shape=jax.ShapeDtypeStruct(pool.shape, pool.dtype),
        in_specs=[SMEM, SMEM, VMEM, VMEM],
        out_specs=VMEM,
        name="keep",
    )(place, plan, pool, swap(leaving))
    return (mixed, final, stored)


def solution(mesh):
    placed = (
        P(None, None, "tensor"),
        P("section", None, None, "tensor"),
        P("section", None, None, "tensor"),
        P("section", "tensor", None),
        P("section", None, "tensor"),
        P("section", "tensor"),
        P("section", None, "tensor"),
        P("section", "tensor"),
        P("section", "tensor"),
        P("section", None, None, "tensor"),
        P(),
        P(),
    )
    return jax.shard_map(
        shards,
        mesh=mesh,
        in_specs=placed,
        out_specs=(
            P("section", None, None, "tensor"),
            P("section", None, None, "tensor"),
            P("section", None, None, "tensor"),
        ),
        check_vma=False,
    )
```

```python
import functools

import jax
import jax.numpy as jnp
from jax import lax
from jax.experimental import pallas as pl
from jax.experimental.pallas import tpu as pltpu
from jax.sharding import PartitionSpec as P

ROWS = 16
LANES = 128
COLS = 512
DEPTH = 1024
ANY = pl.BlockSpec(memory_space=pl.ANY)
HBM = pl.BlockSpec(memory_space=pltpu.HBM)
VMEM = pl.BlockSpec(memory_space=pltpu.VMEM)
SMEM = pl.BlockSpec(memory_space=pltpu.SMEM)
LOG2E = 1.4426950408889634


def softplus(value):
    small = jnp.exp(-jnp.abs(value))
    return jnp.maximum(value, 0.0) + jnp.where(
        small < 1e-3, small - 0.5 * small * small, jnp.log(1.0 + small)
    )


def finish(total, squares, rank):
    rows, width = total.shape
    extra = width - rank
    lane = lax.broadcasted_iota(jnp.int32, (rows, LANES), 1)
    high = squares.astype(jnp.bfloat16).astype(jnp.float32)
    tail = jnp.concatenate(
        [total[:, rank:], jnp.zeros((rows, LANES - extra), jnp.float32)], axis=1
    )
    tail = jnp.where(lane == extra, high, jnp.where(lane == extra + 1, squares - high, tail))
    return total[:, :rank].astype(jnp.bfloat16), tail.astype(jnp.bfloat16)


def open_kernel(meta, inputs, weight, gain, first, rest, block, held, total, sums, sems):
    steps, requests, channels = block.shape
    rank = first.shape[1] - LANES
    depth = min(DEPTH, channels)
    parts = channels // depth

    @pl.when(meta[0] == 0)
    def _():
        copies = []
        for k in range(parts):
            span = pl.ds(k * depth, depth)
            copies.append(
                (
                    pltpu.make_async_copy(weight.at[:, span], held.at[:, span], sems.at[0, k]),
                    pltpu.make_async_copy(
                        inputs.at[:, :, span], block.at[:, :, span], sems.at[1, k]
                    ),
                )
            )
            for copy in copies[-1]:
                copy.start()
        for k in range(parts):
            span = pl.ds(k * depth, depth)
            for copy in copies[k]:
                copy.wait()
            for t in range(steps):
                here = pl.ds(t * requests, requests)
                wide = block[t, :, span].astype(jnp.float32)
                squares = jnp.sum(wide * wide, axis=1, keepdims=True)
                product = lax.dot_general(
                    (wide * gain[:, span]).astype(jnp.bfloat16),
                    held[:, span],
                    (((1,), (1,)), ((), ())),
                    preferred_element_type=jnp.float32,
                )
                squares = jnp.broadcast_to(squares, (requests, LANES))
                total[here, :] = product if k == 0 else total[here, :] + product
                sums[here, :] = squares if k == 0 else sums[here, :] + squares
        for t in range(steps):
            here = pl.ds(t * requests, requests)
            low, tail = finish(total[here, :], sums[here, :1], rank)
            for unit in range(requests // ROWS):
                out = first if unit == 0 else rest
                start = max(unit - 1, 0) * steps * ROWS + t * ROWS
                out[start : start + ROWS, :rank] = low[unit * ROWS : (unit + 1) * ROWS]
                out[start : start + ROWS, rank:] = tail[unit * ROWS : (unit + 1) * ROWS]


def step_kernel(width, layers, peers, *refs):
    meta, plan, arrived = refs[:3]
    near, *others = refs[3 : 3 + peers]
    opening = refs[3 + peers : 3 + 2 * peers]
    (
        inputs,
        state,
        landed,
        dt_weight,
        dt_bias,
        rates,
        skip,
        gain,
        next_gain,
        gate,
        even_weight,
        odd_weight,
        final_in,
        mixed_in,
        leaving_in,
        onward,
        partial,
        final,
        mixed,
        leaving,
        stream,
        terms,
        gates,
        result,
        hold,
        held,
        weight,
        coming,
        going,
        size_rows,
        drive_rows,
        product,
        spread_in,
        spread_out,
        stream_sem,
        term_sem,
        gate_sem,
        state_sem,
        held_sem,
        weight_sem,
        final_sem,
        mixed_sem,
        coming_sem,
        going_sem,
    ) = refs[3 + 2 * peers :]
    steps, rows, channels = gates.shape
    units = steps * rows
    rank = dt_weight.shape[1]
    states = rates.shape[0]
    swaps = going.shape[0]
    cols = min(COLS, channels)
    parts = channels // cols
    depth = min(DEPTH, channels)
    layer = meta[2]

    @pl.when(meta[0] == 1)
    def _():
        first = pl.multiple_of(meta[1], ROWS)
        offset = pl.multiple_of(meta[3], ROWS)

        def planned(which, row, k):
            return plan[((which * 3 + row) * layers + layer) * swaps + k]

        def at(j):
            return pl.ds(pl.multiple_of(j * cols, cols), cols)

        gate_copy = pltpu.make_async_copy(gate.at[0, :, pl.ds(first, rows)], gates, gate_sem)

        def stream_copy(t, fresh):
            if fresh:
                source = inputs.at[t, pl.ds(first, rows)]
            else:
                source = arrived.at[pl.ds(t * rows, rows)]
            return pltpu.make_async_copy(
                source, stream.at[pl.ds(t * rows, rows)], stream_sem.at[t]
            )

        def term_copy(k, fresh):
            if fresh:
                source = opening[k].at[pl.ds(offset, units)]
            else:
                source = others[k - 1] if k else near
            return pltpu.make_async_copy(source, terms.at[k], term_sem.at[k])

        def held_copy(j):
            return pltpu.make_async_copy(
                dt_weight.at[0, :, at(j)], held.at[:, at(j)], held_sem.at[j]
            )

        def weight_copy(k, odd):
            span = pl.ds(k * depth, depth)
            source = odd_weight if odd else even_weight
            return pltpu.make_async_copy(
                source.at[:, span], weight.at[:, span], weight_sem.at[k]
            )

        def state_copy(j):
            return pltpu.make_async_copy(
                state.at[0, pl.ds(first, rows), :, at(j)], hold.at[:, :, at(j)], state_sem.at[j]
            )

        def final_copy(j):
            return pltpu.make_async_copy(
                hold.at[:, :, at(j)], final.at[0, pl.ds(first, rows), :, at(j)], final_sem.at[j]
            )

        def mixed_copy(j):
            return pltpu.make_async_copy(
                result.at[:, :, at(j)], mixed.at[0, :, pl.ds(first, rows), at(j)], mixed_sem.at[j]
            )

        def coming_copy(k):
            return pltpu.make_async_copy(
                landed.at[planned(0, 1, k)], coming.at[k], coming_sem.at[k]
            )

        def going_copy(k):
            return pltpu.make_async_copy(
                going.at[k], leaving.at[planned(1, 1, k)], going_sem.at[k]
            )

        def inside(which, k):
            place = planned(which, 0, k) - first
            return (place >= 0) & (place < rows)

        @pl.when(layer == 0)
        def _():
            for k in range(peers):
                term_copy(k, True).start()
            for t in range(steps):
                stream_copy(t, True).start()

        @pl.when(layer > 0)
        def _():
            for k in range(peers):
                term_copy(k, False).start()
            for t in range(steps):
                stream_copy(t, False).start()

        gate_copy.start()
        for k in range(swaps):

            @pl.when(inside(0, k))
            def _():
                coming_copy(k).start()

        for j in range(parts):
            held_copy(j).start()
            state_copy(j).start()

        @pl.when(layer % 2 == 0)
        def _():
            for k in range(channels // depth):
                weight_copy(k, False).start()

        @pl.when(layer % 2 == 1)
        def _():
            for k in range(channels // depth):
                weight_copy(k, True).start()

        for k in range(peers):
            term_copy(k, False).wait()
        total = jnp.sum(terms[...].astype(jnp.float32), axis=0)
        tail = total[:, rank:]
        squares = tail[:, 2 * states : 2 * states + 1] + tail[:, 2 * states + 1 : 2 * states + 2]
        inverse = 1.0 / jnp.sqrt(squares / width + 1e-05)
        low = (total[:, :rank] * inverse).astype(jnp.bfloat16)
        turned = (tail * inverse).T
        for row in range(units):
            column = turned[: 2 * states, row : row + 1]
            wide = jnp.broadcast_to(column, (2 * states, LANES)).astype(jnp.bfloat16)
            spread_in[row] = wide[:states]
            spread_out[row] = wide[states:]
        gather = (
            lax.broadcasted_iota(jnp.int32, (rows, rows * states), 1) // states
            == lax.broadcasted_iota(jnp.int32, (rows, rows * states), 0)
        ).astype(jnp.bfloat16)
        for k in range(swaps):

            @pl.when(inside(0, k))
            def _():
                coming_copy(k).wait()

        for t in range(steps):
            stream_copy(t, False).wait()
        gate_copy.wait()

        def part(j, carry):
            here = at(j)
            held_copy(j).wait()
            size = softplus(
                jnp.dot(low, held[:, here], preferred_element_type=jnp.float32) + dt_bias[:, here]
            )
            wide = stream[:, here].astype(jnp.float32)
            normed = wide * gain[:, here] * inverse
            size_rows[...] = size
            drive_rows[...] = size * normed
            state_copy(j).wait()
            for k in range(swaps):
                place = planned(0, 0, k) - first

                @pl.when((place >= 0) & (place < rows))
                def _():
                    hold[place, :, here] = coming[k, :, here].astype(jnp.float32)

            rate = rates[:, here]
            for r in range(rows):
                h = hold[r, :, here].astype(jnp.bfloat16)
                for t in range(steps):
                    row = t * rows + r
                    size_row = jnp.broadcast_to(
                        size_rows[row : row + 1, :], (states, cols)
                    ).astype(jnp.bfloat16)
                    drive_row = jnp.broadcast_to(
                        drive_rows[row : row + 1, :], (states, cols)
                    ).astype(jnp.bfloat16)
                    b = jnp.concatenate([spread_in[row]] * (cols // LANES), axis=1)
                    c = jnp.concatenate([spread_out[row]] * (cols // LANES), axis=1)
                    h = jnp.exp2(size_row * rate) * h + drive_row * b
                    product[t, r * states : (r + 1) * states, :] = h * c
                hold[r, :, here] = h.astype(jnp.float32)
            final_copy(j).start()
            for k in range(swaps):
                place = planned(1, 0, k) - first

                @pl.when((place >= 0) & (place < rows))
                def _():
                    going[k, :, here] = hold[place, :, here].astype(jnp.bfloat16)

            summed = jnp.concatenate(
                [
                    jnp.dot(gather, product[t], preferred_element_type=jnp.float32)
                    for t in range(steps)
                ],
                axis=0,
            )
            opened = gates[:, :, here].astype(jnp.float32).reshape(units, cols)
            value = (summed + skip[:, here] * normed) * (opened * jax.nn.sigmoid(opened))
            value = value.astype(jnp.bfloat16)
            result[:, :, here] = value.reshape(steps, rows, cols)
            mixed_copy(j).start()

            onward[:, here] = (wide + value.astype(jnp.float32)).astype(jnp.bfloat16)
            return carry

        lax.fori_loop(0, parts, part, 0)
        for k in range(swaps):
            place = planned(1, 0, k) - first

            @pl.when((place >= 0) & (place < rows))
            def _():
                going_copy(k).start()
                going_copy(k).wait()

        total = jnp.zeros((units, weight.shape[0]), jnp.float32)
        squares = jnp.zeros((units, 1), jnp.float32)
        for k in range(channels // depth):
            span = pl.ds(k * depth, depth)
            wide = onward[:, span].astype(jnp.float32)
            squares += jnp.sum(wide * wide, axis=1, keepdims=True)
            scaled = (wide * next_gain[:, span]).astype(jnp.bfloat16)
            weight_copy(k, False).wait()
            total += lax.dot_general(
                scaled,
                weight[:, span],
                (((1,), (1,)), ((), ())),
                preferred_element_type=jnp.float32,
            )
        low, tail = finish(total, squares, rank)
        partial[:, :rank] = low
        partial[:, rank:] = tail
        for j in range(parts):
            mixed_copy(j).wait()
            final_copy(j).wait()


def pick_kernel(meta, plan, store, out):
    layers = out.shape[0]
    swaps = plan.shape[0] // (6 * layers)
    for layer in range(layers):
        slot = 0
        for k in range(swaps):
            asked = plan[(layers + layer) * swaps + k] == meta[0]
            slot = jnp.where(asked, plan[(2 * layers + layer) * swaps + k], slot)
        out[layer] = store[0, slot].astype(out.dtype)


def keep_kernel(meta, plan, store, returned, out):
    layers = returned.shape[0]
    swaps = plan.shape[0] // (6 * layers)
    for slot in range(store.shape[1]):
        source = -1
        for layer in range(layers):
            for k in range(swaps):
                named = (plan[(4 * layers + layer) * swaps + k] == meta[0]) & (
                    plan[(5 * layers + layer) * swaps + k] == slot
                )
                source = jnp.where(named, layer, source)

        @pl.when(source >= 0)
        def _():
            out[0, slot] = returned[source].astype(out.dtype)

        @pl.when(source < 0)
        def _():
            out[0, slot] = store[0, slot]


def leave(*refs):
    pass


def empty(shapes):
    return pl.pallas_call(leave, out_shape=shapes, out_specs=[HBM] * len(shapes))()


def shards(
    inputs,
    state,
    pool,
    x_weight,
    dt_weight,
    dt_bias,
    a_log,
    skip,
    gain,
    gate_input,
    swap_plan,
    evict_plan,
):
    section = lax.axis_index("section")
    holders = lax.axis_size("section")
    peers = lax.axis_size("tensor")
    channels = x_weight.shape[1]
    width = channels * peers
    rank = dt_weight.shape[1]
    states = a_log.shape[1]
    requests = state.shape[1]
    steps = inputs.shape[0]
    swaps = swap_plan.shape[2]
    units = requests // ROWS
    rows = steps * ROWS
    cols = min(COLS, channels)
    parts = channels // cols
    turns = units + holders - 1
    plan = jnp.concatenate([swap_plan.reshape(-1), evict_plan.reshape(-1)])
    weight = jnp.swapaxes(x_weight[0], 0, 1)
    even = [(i + 1, i) for i in range(0, holders - 1, 2)]
    odd = [(i + 1, i) for i in range(1, holders - 1, 2)]
    odd_weight = lax.ppermute(weight, "section", odd)
    even_weight = lax.ppermute(weight, "section", even)
    next_gain = lax.ppermute(gain, "section", even + odd)
    rates = (-LOG2E * jnp.exp(a_log[0])).astype(jnp.bfloat16)
    place = section.astype(jnp.int32)[None]
    onto = [(i, i + 1) for i in range(holders - 1)]

    block_shape = jax.ShapeDtypeStruct((rows, channels), jnp.bfloat16)
    partial_shape = jax.ShapeDtypeStruct((rows, rank + LANES), jnp.bfloat16)
    rest_shape = jax.ShapeDtypeStruct(((units - 1) * rows, rank + LANES), jnp.bfloat16)
    stream_shape = (steps, ROWS, channels)
    state_shape = jax.ShapeDtypeStruct(state.shape, state.dtype)
    mixed_shape = jax.ShapeDtypeStruct(gate_input.shape, gate_input.dtype)
    moved_shape = jax.ShapeDtypeStruct((holders, states, channels), jnp.bfloat16)
    depth = min(DEPTH, channels)

    def meta_of(turn):
        unit = turn - section
        valid = (unit >= 0) & (unit < units)
        unit = jnp.clip(unit, 0, units - 1)
        return jnp.stack(
            [valid, unit * ROWS, section, jnp.maximum(unit - 1, 0) * rows]
        ).astype(jnp.int32)

    def around(block):
        size = range(peers)
        return [block] + [
            lax.ppermute(block, "tensor", [(i, (i + shift) % peers) for i in size])
            for shift in range(1, peers)
        ]

    def step(meta, blocks, opening, weights, final, mixed, leaving):
        given = 3 + 2 * peers
        return pl.pallas_call(
            functools.partial(step_kernel, width, holders, peers),
            out_shape=[block_shape, partial_shape, state_shape, mixed_shape, moved_shape],
            in_specs=[SMEM, SMEM]
            + [ANY] * (2 * peers + 1)
            + [HBM, HBM, ANY, ANY]
            + [VMEM] * 5
            + [HBM, ANY, ANY]
            + [HBM] * 3,
            out_specs=[VMEM, VMEM, HBM, HBM, HBM],
            scratch_shapes=[
                pltpu.VMEM(block_shape.shape, jnp.bfloat16),
                pltpu.VMEM((peers, *partial_shape.shape), jnp.bfloat16),
                pltpu.VMEM(stream_shape, jnp.bfloat16),
                pltpu.VMEM(stream_shape, jnp.bfloat16),
                pltpu.VMEM((ROWS, states, channels), jnp.float32),
                pltpu.VMEM((rank, channels), jnp.bfloat16),
                pltpu.VMEM(weight.shape, jnp.bfloat16),
                pltpu.VMEM((swaps, states, channels), jnp.bfloat16),
                pltpu.VMEM((swaps, states, channels), jnp.bfloat16),
                pltpu.VMEM((rows, cols), jnp.float32),
                pltpu.VMEM((rows, cols), jnp.float32),
                pltpu.VMEM((steps, ROWS * states, cols), jnp.bfloat16),
                pltpu.VMEM((rows, states, LANES), jnp.bfloat16),
                pltpu.VMEM((rows, states, LANES), jnp.bfloat16),
                pltpu.SemaphoreType.DMA((steps,)),
                pltpu.SemaphoreType.DMA((peers,)),
                pltpu.SemaphoreType.DMA,
                pltpu.SemaphoreType.DMA((parts,)),
                pltpu.SemaphoreType.DMA((parts,)),
                pltpu.SemaphoreType.DMA((channels // depth,)),
                pltpu.SemaphoreType.DMA((parts,)),
                pltpu.SemaphoreType.DMA((parts,)),
                pltpu.SemaphoreType.DMA((swaps,)),
                pltpu.SemaphoreType.DMA((swaps,)),
            ],
            input_output_aliases={given + 12 + k: 2 + k for k in range(3)},
            compiler_params=pltpu.CompilerParams(vmem_limit_bytes=28 * 2**20),
            cost_estimate=pl.CostEstimate(
                flops=4 * rows * channels * (rank + LANES) + 8 * rows * states * channels,
                bytes_accessed=4 * channels * rank + 8 * ROWS * states * channels,
                transcendentals=rows * states * channels,
            ),
            name="step",
        )(
            meta,
            plan,
            *blocks,
            *opening,
            inputs,
            state,
            landed,
            dt_weight,
            dt_bias,
            rates,
            skip,
            gain,
            next_gain,
            gate_input,
            *weights,
            final,
            mixed,
            leaving,
        )

    def send(block, partial):
        near = lax.ppermute(partial, "section", onto)
        arrived = lax.ppermute(block, "section", onto)
        return [arrived, *around(near)]

    def swap(block):
        return lax.all_to_all(block, "section", split_axis=0, concat_axis=0, tiled=True)

    def turn(index, carry):
        blocks, kept = carry
        block, partial, *kept = step(
            meta_of(index), blocks, rest, (even_weight, odd_weight), *kept
        )
        return send(block, partial), kept

    picked = pl.pallas_call(
        pick_kernel, out_shape=moved_shape, in_specs=[SMEM, SMEM, VMEM], out_specs=VMEM, name="pick"
    )(place, plan, pool)
    first, rest = pl.pallas_call(
        open_kernel,
        out_shape=[partial_shape, rest_shape],
        in_specs=[SMEM, HBM, HBM, VMEM],
        out_specs=[VMEM, VMEM],
        scratch_shapes=[
            pltpu.VMEM(inputs.shape, jnp.bfloat16),
            pltpu.VMEM(weight.shape, jnp.bfloat16),
            pltpu.VMEM((steps * requests, weight.shape[0]), jnp.float32),
            pltpu.VMEM((steps * requests, LANES), jnp.float32),
            pltpu.SemaphoreType.DMA((2, channels // depth)),
        ],
        compiler_params=pltpu.CompilerParams(vmem_limit_bytes=28 * 2**20),
        name="open",
    )(place, inputs, weight, gain)
    landed = swap(picked)
    first = around(first)
    rest = around(rest)
    *kept, block = empty([state_shape, mixed_shape, moved_shape, block_shape])
    blocks = [block, *first]
    block, partial, *kept = step(meta_of(0), blocks, first, (even_weight, even_weight), *kept)
    blocks, kept = lax.fori_loop(1, turns - 1, turn, (send(block, partial), kept))
    _, _, final, mixed, leaving = step(
        meta_of(turns - 1), blocks, rest, (even_weight, odd_weight), *kept
    )
    stored = pl.pallas_call(
        keep_kernel,
        out_shape=jax.ShapeDtypeStruct(pool.shape, pool.dtype),
        in_specs=[SMEM, SMEM, VMEM, VMEM],
        out_specs=VMEM,
        name="keep",
    )(place, plan, pool, swap(leaving))
    return (mixed, final, stored)


def solution(mesh):
    placed = (
        P(None, None, "tensor"),
        P("section", None, None, "tensor"),
        P("section", None, None, "tensor"),
        P("section", "tensor", None),
        P("section", None, "tensor"),
        P("section", "tensor"),
        P("section", None, "tensor"),
        P("section", "tensor"),
        P("section", "tensor"),
        P("section", None, None, "tensor"),
        P(),
        P(),
    )
    return jax.shard_map(
        shards,
        mesh=mesh,
        in_specs=placed,
        out_specs=(
            P("section", None, None, "tensor"),
            P("section", None, None, "tensor"),
            P("section", None, None, "tensor"),
        ),
        check_vma=False,
    )
```

```python
import functools

import jax
import jax.numpy as jnp
from jax import lax
from jax.experimental import pallas as pl
from jax.experimental.pallas import tpu as pltpu
from jax.sharding import PartitionSpec as P

ROWS = 16
LANES = 128
COLS = 512
DEPTH = 1024
ANY = pl.BlockSpec(memory_space=pl.ANY)
HBM = pl.BlockSpec(memory_space=pltpu.HBM)
VMEM = pl.BlockSpec(memory_space=pltpu.VMEM)
SMEM = pl.BlockSpec(memory_space=pltpu.SMEM)
LOG2E = 1.4426950408889634


def softplus(value):
    small = jnp.exp(-jnp.abs(value))
    return jnp.maximum(value, 0.0) + jnp.where(
        small < 1e-3, small - 0.5 * small * small, jnp.log(1.0 + small)
    )


def finish(total, squares, rank):
    rows, width = total.shape
    extra = width - rank
    lane = lax.broadcasted_iota(jnp.int32, (rows, LANES), 1)
    high = squares.astype(jnp.bfloat16).astype(jnp.float32)
    tail = jnp.concatenate(
        [total[:, rank:], jnp.zeros((rows, LANES - extra), jnp.float32)], axis=1
    )
    tail = jnp.where(lane == extra, high, jnp.where(lane == extra + 1, squares - high, tail))
    return total[:, :rank].astype(jnp.bfloat16), tail.astype(jnp.bfloat16)


def merge(even, odd, sublane, distance):
    clear = (sublane & distance) == 0
    size = sublane.shape[0]
    near = jnp.where(clear, even, pltpu.roll(odd, distance, 0))
    far = jnp.where(clear, pltpu.roll(even, size - distance, 0), odd)
    return near + far


def step_kernel(width, layers, peers, *refs):
    meta, plan, arrived = refs[:3]
    others = refs[3 : 2 + peers]
    (
        inputs,
        state,
        landed,
        dt_weight,
        dt_bias,
        rates,
        skip,
        gain,
        next_gain,
        gate,
        next_weight,
        final_in,
        mixed_in,
        leaving_in,
        onward,
        partial,
        final,
        mixed,
        leaving,
        gates,
        result,
        hold,
        held,
        weight,
        coming,
        going,
        size_rows,
        drive_rows,
        base_rows,
        totals,
        spread_in,
        spread_out,
        input_sem,
        gate_sem,
        state_sem,
        held_sem,
        weight_sem,
        final_sem,
        mixed_sem,
        coming_sem,
        going_sem,
    ) = refs[2 + peers :]
    steps, rows, channels = gates.shape
    units = steps * rows
    rank = dt_weight.shape[1]
    states = rates.shape[0]
    swaps = going.shape[0]
    cols = min(COLS, channels)
    parts = channels // cols
    depth = min(DEPTH, channels)
    wide_lanes = min(2 * LANES, cols)
    layer = meta[2]
    ahead = (meta[3] == 1) & (layer == layers - 1)
    first = pl.multiple_of(meta[1], ROWS)

    def at(j):
        return pl.ds(pl.multiple_of(j * cols, cols), cols)

    def input_copy(t):
        return pltpu.make_async_copy(
            inputs.at[t, pl.ds(pl.multiple_of(meta[4], ROWS), rows)],
            onward.at[pl.ds(t * rows, rows), pl.ds(0, channels)],
            input_sem.at[t],
        )

    def weight_copy(k):
        span = pl.ds(k * depth, depth)
        return pltpu.make_async_copy(next_weight.at[:, span], weight.at[:, span], weight_sem.at[k])

    def final_copy(j):
        return pltpu.make_async_copy(
            hold.at[:, :, at(j)], final.at[0, pl.ds(first, rows), :, at(j)], final_sem.at[j]
        )

    def mixed_copy(j):
        return pltpu.make_async_copy(
            result.at[:, :, at(j)], mixed.at[0, :, pl.ds(first, rows), at(j)], mixed_sem.at[j]
        )

    @pl.when(ahead)
    def _():
        for t in range(steps):
            input_copy(t).start()

    @pl.when((meta[3] == 1) & (meta[0] == 0))
    def _():
        for k in range(channels // depth):
            weight_copy(k).start()

    @pl.when(meta[0] == 1)
    def _():
        def planned(which, row, k):
            return plan[((which * 3 + row) * layers + layer) * swaps + k]

        gate_copy = pltpu.make_async_copy(gate.at[0, :, pl.ds(first, rows)], gates, gate_sem)

        def held_copy(j):
            return pltpu.make_async_copy(
                dt_weight.at[0, :, at(j)], held.at[:, at(j)], held_sem.at[j]
            )

        def state_copy(j):
            return pltpu.make_async_copy(
                state.at[0, pl.ds(first, rows), :, at(j)], hold.at[:, :, at(j)], state_sem.at[j]
            )

        def coming_copy(k):
            return pltpu.make_async_copy(
                landed.at[planned(0, 1, k)], coming.at[k], coming_sem.at[k]
            )

        def going_copy(k):
            return pltpu.make_async_copy(
                going.at[k], leaving.at[planned(1, 1, k)], going_sem.at[k]
            )

        def inside(which, k):
            place = planned(which, 0, k) - first
            return (place >= 0) & (place < rows)

        gate_copy.start()
        for k in range(swaps):

            @pl.when(inside(0, k))
            def _():
                coming_copy(k).start()

        for j in range(parts):
            held_copy(j).start()
            state_copy(j).start()

        @pl.when(meta[3] == 1)
        def _():
            for k in range(channels // depth):
                weight_copy(k).start()

        total = arrived[:, channels:].astype(jnp.float32)
        for other in others:
            total += other[...].astype(jnp.float32)
        tail = total[:, rank:]
        squares = tail[:, 2 * states : 2 * states + 1] + tail[:, 2 * states + 1 : 2 * states + 2]
        inverse = 1.0 / jnp.sqrt(squares / width + 1e-05)
        low = (total[:, :rank] * inverse).astype(jnp.bfloat16)
        turned = (tail * inverse).T
        for row in range(units):
            column = turned[: 2 * states, row : row + 1]
            wide = jnp.broadcast_to(column, (2 * states, LANES)).astype(jnp.bfloat16)
            spread_in[row] = wide[:states]
            spread_out[row] = wide[states:]
        sublane = lax.broadcasted_iota(jnp.int32, (states // 2, wide_lanes), 0)
        for k in range(swaps):

            @pl.when(inside(0, k))
            def _():
                coming_copy(k).wait()

        gate_copy.wait()

        def prepare(j, slot):
            here = at(j)
            size = softplus(
                jnp.dot(low, held[:, here], preferred_element_type=jnp.float32) + dt_bias[:, here]
            )
            normed = arrived[:, here].astype(jnp.float32) * gain[:, here] * inverse
            size_rows[slot] = size
            drive_rows[slot] = size * normed
            base_rows[slot] = skip[:, here] * normed

        held_copy(0).wait()
        prepare(0, 0)

        def part(j, carry):
            here = at(j)
            slot = lax.rem(j, 2)
            later = jnp.minimum(j + 1, parts - 1)
            state_copy(j).wait()

            @pl.when(j + 1 < parts)
            def _():
                held_copy(j + 1).wait()

            for k in range(swaps):
                place = planned(0, 0, k) - first

                @pl.when((place >= 0) & (place < rows))
                def _():
                    hold[place, :, here] = coming[k, :, here].astype(jnp.float32)

            for strip in range(cols // wide_lanes):
                lanes = pl.ds(strip * wide_lanes, wide_lanes)
                full = pl.ds(pl.multiple_of(j * cols + strip * wide_lanes, LANES), wide_lanes)
                rate = rates[:, full]
                pending = {}
                for r in range(rows):
                    h = hold[r, :, full].astype(jnp.bfloat16)
                    for t in range(steps):
                        row = t * rows + r
                        size_row = jnp.broadcast_to(
                            size_rows[slot, row : row + 1, lanes], (states, wide_lanes)
                        ).astype(jnp.bfloat16)
                        drive_row = jnp.broadcast_to(
                            drive_rows[slot, row : row + 1, lanes], (states, wide_lanes)
                        ).astype(jnp.bfloat16)
                        b = jnp.concatenate([spread_in[row]] * (wide_lanes // LANES), axis=1)
                        c = jnp.concatenate([spread_out[row]] * (wide_lanes // LANES), axis=1)
                        h = jnp.exp2(size_row * rate) * h + drive_row * b
                        term = (h * c).astype(jnp.float32)
                        term = term[: states // 2] + term[states // 2 :]
                        distance = 1
                        while (t, distance) in pending:
                            term = merge(pending.pop((t, distance)), term, sublane, distance)
                            distance *= 2
                        if distance == states // 2:
                            start = row - row % (states // 2)
                            totals[start : start + states // 2, lanes] = term
                        else:
                            pending[t, distance] = term
                    hold[r, :, full] = h.astype(jnp.float32)

            opened = gates[:, :, here].astype(jnp.float32).reshape(units, cols)
            value = (totals[...] + base_rows[slot]) * (opened * jax.nn.sigmoid(opened))
            value = value.astype(jnp.bfloat16)
            result[:, :, here] = value.reshape(steps, rows, cols)
            passed = arrived[:, here].astype(jnp.float32) + value.astype(jnp.float32)
            passed = passed.astype(jnp.bfloat16)
            prepare(later, 1 - slot)

            @pl.when(layer < layers - 1)
            def _():
                onward[:, here] = passed

            final_copy(j).start()
            mixed_copy(j).start()
            return carry

        lax.fori_loop(0, parts, part, 0)
        for k in range(swaps):
            place = planned(1, 0, k) - first

            @pl.when((place >= 0) & (place < rows))
            def _():
                going[k] = hold[place].astype(jnp.bfloat16)
                going_copy(k).start()
                going_copy(k).wait()

    @pl.when(ahead)
    def _():
        for t in range(steps):
            input_copy(t).wait()

    @pl.when(meta[3] == 1)
    def _():
        total = jnp.zeros((units, weight.shape[0]), jnp.float32)
        squares = jnp.zeros((units, 1), jnp.float32)
        for k in range(channels // depth):
            span = pl.ds(k * depth, depth)
            wide = onward[:, span].astype(jnp.float32)
            squares += jnp.sum(wide * wide, axis=1, keepdims=True)
            scaled = (wide * next_gain[:, span]).astype(jnp.bfloat16)
            weight_copy(k).wait()
            total += lax.dot_general(
                scaled,
                weight[:, span],
                (((1,), (1,)), ((), ())),
                preferred_element_type=jnp.float32,
            )
        low, tail = finish(total, squares, rank)
        onward[:, channels : channels + rank] = low
        onward[:, channels + rank :] = tail
        partial[:, :rank] = low
        partial[:, rank:] = tail

    @pl.when(meta[0] == 1)
    def _():
        for j in range(parts):
            mixed_copy(j).wait()
            final_copy(j).wait()


def pick_kernel(meta, plan, store, out):
    layers = out.shape[0]
    swaps = plan.shape[0] // (6 * layers)
    for layer in range(layers):
        slot = 0
        for k in range(swaps):
            asked = plan[(layers + layer) * swaps + k] == meta[0]
            slot = jnp.where(asked, plan[(2 * layers + layer) * swaps + k], slot)
        out[layer] = store[0, slot].astype(out.dtype)


def keep_kernel(meta, plan, store, returned, out):
    layers = returned.shape[0]
    swaps = plan.shape[0] // (6 * layers)
    for slot in range(store.shape[1]):
        source = -1
        for layer in range(layers):
            for k in range(swaps):
                named = (plan[(4 * layers + layer) * swaps + k] == meta[0]) & (
                    plan[(5 * layers + layer) * swaps + k] == slot
                )
                source = jnp.where(named, layer, source)

        @pl.when(source >= 0)
        def _():
            out[0, slot] = returned[source].astype(out.dtype)

        @pl.when(source < 0)
        def _():
            out[0, slot] = store[0, slot]


def leave(*refs):
    pass


def empty(shapes):
    return pl.pallas_call(leave, out_shape=shapes, out_specs=[HBM] * len(shapes))()


def shards(
    inputs,
    state,
    pool,
    x_weight,
    dt_weight,
    dt_bias,
    a_log,
    skip,
    gain,
    gate_input,
    swap_plan,
    evict_plan,
):
    section = lax.axis_index("section")
    holders = lax.axis_size("section")
    peers = lax.axis_size("tensor")
    channels = x_weight.shape[1]
    width = channels * peers
    rank = dt_weight.shape[1]
    states = a_log.shape[1]
    requests = state.shape[1]
    steps = inputs.shape[0]
    swaps = swap_plan.shape[2]
    pairs = requests // (2 * ROWS)
    rows = steps * ROWS
    cols = min(COLS, channels)
    parts = channels // cols
    depth = min(DEPTH, channels)
    turns = pairs + holders - 1
    plan = jnp.concatenate([swap_plan.reshape(-1), evict_plan.reshape(-1)])
    down = [((i + 1) % holders, i) for i in range(holders)]
    weight = lax.ppermute(jnp.swapaxes(x_weight[0], 0, 1), "section", down)
    next_gain = lax.ppermute(gain, "section", down)
    rates = (-LOG2E * jnp.exp(a_log[0])).astype(jnp.bfloat16)
    place = section.astype(jnp.int32)[None]

    block_shape = jax.ShapeDtypeStruct((rows, channels + rank + LANES), jnp.bfloat16)
    partial_shape = jax.ShapeDtypeStruct((rows, rank + LANES), jnp.bfloat16)
    stream_shape = (steps, ROWS, channels)
    state_shape = jax.ShapeDtypeStruct(state.shape, state.dtype)
    mixed_shape = jax.ShapeDtypeStruct(gate_input.shape, gate_input.dtype)
    moved_shape = jax.ShapeDtypeStruct((holders, states, channels), jnp.bfloat16)

    def meta_of(turn, half):
        pair = turn - section
        valid = (pair >= 0) & (pair < pairs)
        last = section == holders - 1
        following = turn + 1
        ahead = jnp.where(last, (following >= 0) & (following < pairs), valid)
        first = (jnp.clip(pair, 0, pairs - 1) * 2 + half) * ROWS
        then = (jnp.clip(following, 0, pairs - 1) * 2 + half) * ROWS
        return jnp.stack([valid, first, section, ahead, then]).astype(jnp.int32)

    def step(meta, blocks, final, mixed, leaving):
        given = 2 + peers
        return pl.pallas_call(
            functools.partial(step_kernel, width, holders, peers),
            out_shape=[block_shape, partial_shape, state_shape, mixed_shape, moved_shape],
            in_specs=[SMEM, SMEM]
            + [VMEM] * peers
            + [HBM, HBM, ANY, ANY]
            + [VMEM] * 5
            + [HBM, ANY]
            + [HBM] * 3,
            out_specs=[VMEM, VMEM, HBM, HBM, HBM],
            scratch_shapes=[
                pltpu.VMEM(stream_shape, jnp.bfloat16),
                pltpu.VMEM(stream_shape, jnp.bfloat16),
                pltpu.VMEM((ROWS, states, channels), jnp.float32),
                pltpu.VMEM((rank, channels), jnp.bfloat16),
                pltpu.VMEM(weight.shape, jnp.bfloat16),
                pltpu.VMEM((swaps, states, channels), jnp.bfloat16),
                pltpu.VMEM((swaps, states, channels), jnp.bfloat16),
                pltpu.VMEM((2, rows, cols), jnp.float32),
                pltpu.VMEM((2, rows, cols), jnp.float32),
                pltpu.VMEM((2, rows, cols), jnp.float32),
                pltpu.VMEM((rows, cols), jnp.float32),
                pltpu.VMEM((rows, states, LANES), jnp.bfloat16),
                pltpu.VMEM((rows, states, LANES), jnp.bfloat16),
                pltpu.SemaphoreType.DMA((steps,)),
                pltpu.SemaphoreType.DMA,
                pltpu.SemaphoreType.DMA((parts,)),
                pltpu.SemaphoreType.DMA((parts,)),
                pltpu.SemaphoreType.DMA((channels // depth,)),
                pltpu.SemaphoreType.DMA((parts,)),
                pltpu.SemaphoreType.DMA((parts,)),
                pltpu.SemaphoreType.DMA((swaps,)),
                pltpu.SemaphoreType.DMA((swaps,)),
            ],
            input_output_aliases={given + 11 + k: 2 + k for k in range(3)},
            compiler_params=pltpu.CompilerParams(vmem_limit_bytes=28 * 2**20),
            cost_estimate=pl.CostEstimate(
                flops=4 * rows * channels * (rank + LANES) + 8 * rows * states * channels,
                bytes_accessed=4 * channels * rank + 8 * ROWS * states * channels,
                transcendentals=rows * states * channels,
            ),
            name="step",
        )(
            meta,
            plan,
            *blocks,
            inputs,
            state,
            landed,
            dt_weight,
            dt_bias,
            rates,
            skip,
            gain,
            next_gain,
            gate_input,
            weight,
            final,
            mixed,
            leaving,
        )

    def send(block, partial):
        axes = ("section", "tensor")
        blocks = []
        for shift in range(peers):
            route = [
                (l * peers + i, (l + 1) % holders * peers + (i + shift) % peers)
                for l in range(holders)
                for i in range(peers)
            ]
            blocks.append(lax.ppermute(partial if shift else block, axes, route))
        return blocks

    def swap(block):
        return lax.all_to_all(block, "section", split_axis=0, concat_axis=0, tiled=True)

    def turn(index, carry):
        out, late, kept = carry
        early = send(*out)
        *out, final, mixed, leaving = step(meta_of(index - 1, 1), late, *kept)
        late = send(*out)
        *out, final, mixed, leaving = step(meta_of(index, 0), early, final, mixed, leaving)
        return tuple(out), tuple(late), (final, mixed, leaving)

    picked = pl.pallas_call(
        pick_kernel, out_shape=moved_shape, in_specs=[SMEM, SMEM, VMEM], out_specs=VMEM, name="pick"
    )(place, plan, pool)
    landed = swap(picked)
    *kept, block, partial = empty(
        [state_shape, mixed_shape, moved_shape, block_shape, partial_shape]
    )
    late = (block,) + (partial,) * (peers - 1)
    *out, final, mixed, leaving = step(meta_of(-1, 0), late, *kept)
    out, late, kept = lax.fori_loop(
        0, turns, turn, (tuple(out), late, (final, mixed, leaving))
    )
    _, _, final, mixed, leaving = step(meta_of(turns - 1, 1), late, *kept)
    stored = pl.pallas_call(
        keep_kernel,
        out_shape=jax.ShapeDtypeStruct(pool.shape, pool.dtype),
        in_specs=[SMEM, SMEM, VMEM, VMEM],
        out_specs=VMEM,
        name="keep",
    )(place, plan, pool, swap(leaving))
    return (mixed, final, stored)


def solution(mesh):
    placed = (
        P(None, None, "tensor"),
        P("section", None, None, "tensor"),
        P("section", None, None, "tensor"),
        P("section", "tensor", None),
        P("section", None, "tensor"),
        P("section", "tensor"),
        P("section", None, "tensor"),
        P("section", "tensor"),
        P("section", "tensor"),
        P("section", None, None, "tensor"),
        P(),
        P(),
    )
    return jax.shard_map(
        shards,
        mesh=mesh,
        in_specs=placed,
        out_specs=(
            P("section", None, None, "tensor"),
            P("section", None, None, "tensor"),
            P("section", None, None, "tensor"),
        ),
        check_vma=False,
    )
```

```python
import functools

import jax
import jax.numpy as jnp
from jax import lax
from jax.experimental import pallas as pl
from jax.experimental.pallas import tpu as pltpu
from jax.sharding import PartitionSpec as P

ROWS = 16
LANES = 128
COLS = 512
DEPTH = 1024
ANY = pl.BlockSpec(memory_space=pl.ANY)
HBM = pl.BlockSpec(memory_space=pltpu.HBM)
VMEM = pl.BlockSpec(memory_space=pltpu.VMEM)
SMEM = pl.BlockSpec(memory_space=pltpu.SMEM)
LOG2E = 1.4426950408889634


def softplus(value):
    small = jnp.exp(-jnp.abs(value))
    return jnp.maximum(value, 0.0) + jnp.where(
        small < 1e-3, small - 0.5 * small * small, jnp.log(1.0 + small)
    )


def finish(total, squares, rank):
    rows, width = total.shape
    extra = width - rank
    lane = lax.broadcasted_iota(jnp.int32, (rows, LANES), 1)
    high = squares.astype(jnp.bfloat16).astype(jnp.float32)
    tail = jnp.concatenate(
        [total[:, rank:], jnp.zeros((rows, LANES - extra), jnp.float32)], axis=1
    )
    tail = jnp.where(lane == extra, high, jnp.where(lane == extra + 1, squares - high, tail))
    return total[:, :rank].astype(jnp.bfloat16), tail.astype(jnp.bfloat16)


def merge(even, odd, sublane, distance):
    clear = (sublane & distance) == 0
    size = sublane.shape[0]
    near = jnp.where(clear, even, pltpu.roll(odd, distance, 0))
    far = jnp.where(clear, pltpu.roll(even, size - distance, 0), odd)
    return near + far


def step_kernel(width, layers, peers, *refs):
    meta, plan, arrived = refs[:3]
    others = refs[3 : 2 + peers]
    (
        inputs,
        state,
        landed,
        dt_weight,
        dt_bias,
        rates,
        skip,
        gain,
        next_gain,
        gate,
        weight,
        final_in,
        mixed_in,
        leaving_in,
        onward,
        partial,
        final,
        mixed,
        leaving,
        gates,
        result,
        hold,
        coming,
        going,
        size_rows,
        drive_rows,
        base_rows,
        totals,
        spread_in,
        spread_out,
        input_sem,
        gate_sem,
        state_sem,
        final_sem,
        mixed_sem,
        coming_sem,
        going_sem,
    ) = refs[2 + peers :]
    steps, rows, channels = gates.shape
    units = steps * rows
    rank = dt_weight.shape[1]
    states = rates.shape[0]
    swaps = going.shape[0]
    cols = min(COLS, channels)
    parts = channels // cols
    depth = min(DEPTH, channels)
    wide_lanes = min(2 * LANES, cols)
    layer = meta[2]
    ahead = (meta[3] == 1) & (layer == layers - 1)
    first = pl.multiple_of(meta[1], ROWS)

    def at(j):
        return pl.ds(pl.multiple_of(j * cols, cols), cols)

    def input_copy(t):
        return pltpu.make_async_copy(
            inputs.at[t, pl.ds(pl.multiple_of(meta[4], ROWS), rows)],
            onward.at[pl.ds(t * rows, rows), pl.ds(0, channels)],
            input_sem.at[t],
        )

    def final_copy(j):
        return pltpu.make_async_copy(
            hold.at[:, :, at(j)], final.at[0, pl.ds(first, rows), :, at(j)], final_sem.at[j]
        )

    def mixed_copy(j):
        return pltpu.make_async_copy(
            result.at[:, :, at(j)], mixed.at[0, :, pl.ds(first, rows), at(j)], mixed_sem.at[j]
        )

    @pl.when(ahead)
    def _():
        for t in range(steps):
            input_copy(t).start()

    @pl.when(meta[0] == 1)
    def _():
        def planned(which, row, k):
            return plan[((which * 3 + row) * layers + layer) * swaps + k]

        gate_copy = pltpu.make_async_copy(gate.at[0, :, pl.ds(first, rows)], gates, gate_sem)

        def state_copy(j):
            return pltpu.make_async_copy(
                state.at[0, pl.ds(first, rows), :, at(j)], hold.at[:, :, at(j)], state_sem.at[j]
            )

        def coming_copy(k):
            return pltpu.make_async_copy(
                landed.at[planned(0, 1, k)], coming.at[k], coming_sem.at[k]
            )

        def going_copy(k):
            return pltpu.make_async_copy(
                going.at[k], leaving.at[planned(1, 1, k)], going_sem.at[k]
            )

        def inside(which, k):
            place = planned(which, 0, k) - first
            return (place >= 0) & (place < rows)

        gate_copy.start()
        for k in range(swaps):

            @pl.when(inside(0, k))
            def _():
                coming_copy(k).start()

        for j in range(parts):
            state_copy(j).start()

        total = arrived[:, channels:].astype(jnp.float32)
        for other in others:
            total += other[...].astype(jnp.float32)
        tail = total[:, rank:]
        squares = tail[:, 2 * states : 2 * states + 1] + tail[:, 2 * states + 1 : 2 * states + 2]
        inverse = 1.0 / jnp.sqrt(squares / width + 1e-05)
        low = (total[:, :rank] * inverse).astype(jnp.bfloat16)
        turned = (tail * inverse).T
        for row in range(units):
            column = turned[: 2 * states, row : row + 1]
            wide = jnp.broadcast_to(column, (2 * states, LANES))
            spread_in[row] = wide[:states]
            spread_out[row] = wide[states:]
        sublane = lax.broadcasted_iota(jnp.int32, (states // 2, wide_lanes), 0)
        for k in range(swaps):

            @pl.when(inside(0, k))
            def _():
                coming_copy(k).wait()

        gate_copy.wait()

        def prepare(j, slot):
            here = at(j)
            size = softplus(
                jnp.dot(low, dt_weight[0, :, here], preferred_element_type=jnp.float32) + dt_bias[:, here]
            )
            normed = arrived[:, here].astype(jnp.float32) * gain[:, here] * inverse
            size_rows[slot] = size
            drive_rows[slot] = size * normed
            base_rows[slot] = skip[:, here] * normed

        prepare(0, 0)

        def part(j, carry):
            here = at(j)
            slot = lax.rem(j, 2)
            later = jnp.minimum(j + 1, parts - 1)
            state_copy(j).wait()

            for k in range(swaps):
                place = planned(0, 0, k) - first

                @pl.when((place >= 0) & (place < rows))
                def _():
                    hold[place, :, here] = coming[k, :, here].astype(jnp.float32)

            for strip in range(cols // wide_lanes):
                lanes = pl.ds(strip * wide_lanes, wide_lanes)
                full = pl.ds(pl.multiple_of(j * cols + strip * wide_lanes, LANES), wide_lanes)
                rate = rates[:, full]
                pending = {}
                for r in range(rows):
                    h = hold[r, :, full]
                    for t in range(steps):
                        row = t * rows + r
                        size_row = jnp.broadcast_to(
                            size_rows[slot, row : row + 1, lanes], (states, wide_lanes)
                        )
                        drive_row = jnp.broadcast_to(
                            drive_rows[slot, row : row + 1, lanes], (states, wide_lanes)
                        )
                        b = jnp.concatenate([spread_in[row]] * (wide_lanes // LANES), axis=1)
                        c = jnp.concatenate([spread_out[row]] * (wide_lanes // LANES), axis=1)
                        h = jnp.exp2(size_row * rate) * h + drive_row * b
                        term = h * c
                        term = term[: states // 2] + term[states // 2 :]
                        distance = 1
                        while (t, distance) in pending:
                            term = merge(pending.pop((t, distance)), term, sublane, distance)
                            distance *= 2
                        if distance == states // 2:
                            start = row - row % (states // 2)
                            totals[start : start + states // 2, lanes] = term
                        else:
                            pending[t, distance] = term
                    hold[r, :, full] = h

            opened = gates[:, :, here].astype(jnp.float32).reshape(units, cols)
            value = (totals[...] + base_rows[slot]) * (opened * jax.nn.sigmoid(opened))
            value = value.astype(jnp.bfloat16)
            result[:, :, here] = value.reshape(steps, rows, cols)
            passed = arrived[:, here].astype(jnp.float32) + value.astype(jnp.float32)
            passed = passed.astype(jnp.bfloat16)
            prepare(later, 1 - slot)

            @pl.when(layer < layers - 1)
            def _():
                onward[:, here] = passed

            final_copy(j).start()
            mixed_copy(j).start()
            return carry

        lax.fori_loop(0, parts, part, 0)
        for k in range(swaps):
            place = planned(1, 0, k) - first

            @pl.when((place >= 0) & (place < rows))
            def _():
                going[k] = hold[place].astype(jnp.bfloat16)
                going_copy(k).start()
                going_copy(k).wait()

    @pl.when(ahead)
    def _():
        for t in range(steps):
            input_copy(t).wait()

    @pl.when(meta[3] == 1)
    def _():
        total = jnp.zeros((units, weight.shape[0]), jnp.float32)
        squares = jnp.zeros((units, 1), jnp.float32)
        for k in range(channels // depth):
            span = pl.ds(k * depth, depth)
            wide = onward[:, span].astype(jnp.float32)
            squares += jnp.sum(wide * wide, axis=1, keepdims=True)
            scaled = (wide * next_gain[:, span]).astype(jnp.bfloat16)
            total += lax.dot_general(
                scaled,
                weight[:, span],
                (((1,), (1,)), ((), ())),
                preferred_element_type=jnp.float32,
            )
        low, tail = finish(total, squares, rank)
        onward[:, channels : channels + rank] = low
        onward[:, channels + rank :] = tail
        partial[:, :rank] = low
        partial[:, rank:] = tail

    @pl.when(meta[0] == 1)
    def _():
        for j in range(parts):
            mixed_copy(j).wait()
            final_copy(j).wait()


def pick_kernel(meta, plan, store, out):
    layers = out.shape[0]
    swaps = plan.shape[0] // (6 * layers)
    for layer in range(layers):
        slot = 0
        for k in range(swaps):
            asked = plan[(layers + layer) * swaps + k] == meta[0]
            slot = jnp.where(asked, plan[(2 * layers + layer) * swaps + k], slot)
        out[layer] = store[0, slot].astype(out.dtype)


def keep_kernel(meta, plan, store, returned, out):
    layers = returned.shape[0]
    swaps = plan.shape[0] // (6 * layers)
    for slot in range(store.shape[1]):
        source = -1
        for layer in range(layers):
            for k in range(swaps):
                named = (plan[(4 * layers + layer) * swaps + k] == meta[0]) & (
                    plan[(5 * layers + layer) * swaps + k] == slot
                )
                source = jnp.where(named, layer, source)

        @pl.when(source >= 0)
        def _():
            out[0, slot] = returned[source].astype(out.dtype)

        @pl.when(source < 0)
        def _():
            out[0, slot] = store[0, slot]


def leave(*refs):
    pass


def empty(shapes):
    return pl.pallas_call(leave, out_shape=shapes, out_specs=[HBM] * len(shapes))()


def shards(
    inputs,
    state,
    pool,
    x_weight,
    dt_weight,
    dt_bias,
    a_log,
    skip,
    gain,
    gate_input,
    swap_plan,
    evict_plan,
):
    section = lax.axis_index("section")
    holders = lax.axis_size("section")
    peers = lax.axis_size("tensor")
    channels = x_weight.shape[1]
    width = channels * peers
    rank = dt_weight.shape[1]
    states = a_log.shape[1]
    requests = state.shape[1]
    steps = inputs.shape[0]
    swaps = swap_plan.shape[2]
    units = requests // ROWS
    rows = steps * ROWS
    cols = min(COLS, channels)
    parts = channels // cols
    depth = min(DEPTH, channels)
    turns = units + holders - 1
    plan = jnp.concatenate([swap_plan.reshape(-1), evict_plan.reshape(-1)])
    down = [((i + 1) % holders, i) for i in range(holders)]
    weight = lax.ppermute(jnp.swapaxes(x_weight[0], 0, 1), "section", down)
    next_gain = lax.ppermute(gain, "section", down)
    rates = -LOG2E * jnp.exp(a_log[0])
    place = section.astype(jnp.int32)[None]

    block_shape = jax.ShapeDtypeStruct((rows, channels + rank + LANES), jnp.bfloat16)
    partial_shape = jax.ShapeDtypeStruct((rows, rank + LANES), jnp.bfloat16)
    stream_shape = (steps, ROWS, channels)
    state_shape = jax.ShapeDtypeStruct(state.shape, state.dtype)
    mixed_shape = jax.ShapeDtypeStruct(gate_input.shape, gate_input.dtype)
    moved_shape = jax.ShapeDtypeStruct((holders, states, channels), jnp.bfloat16)

    def meta_of(turn):
        unit = turn - section
        valid = (unit >= 0) & (unit < units)
        last = section == holders - 1
        following = turn + 1
        ahead = jnp.where(last, following < units, valid)
        first = jnp.clip(unit, 0, units - 1) * ROWS
        then = jnp.clip(following, 0, units - 1) * ROWS
        return jnp.stack([valid, first, section, ahead, then]).astype(jnp.int32)

    def step(meta, blocks, final, mixed, leaving):
        given = 2 + peers
        return pl.pallas_call(
            functools.partial(step_kernel, width, holders, peers),
            out_shape=[block_shape, partial_shape, state_shape, mixed_shape, moved_shape],
            in_specs=[SMEM, SMEM]
            + [VMEM] * peers
            + [HBM, HBM, ANY]
            + [VMEM] * 6
            + [HBM, VMEM]
            + [HBM] * 3,
            out_specs=[VMEM, VMEM, HBM, HBM, HBM],
            scratch_shapes=[
                pltpu.VMEM(stream_shape, jnp.bfloat16),
                pltpu.VMEM(stream_shape, jnp.bfloat16),
                pltpu.VMEM((ROWS, states, channels), jnp.float32),
                pltpu.VMEM((swaps, states, channels), jnp.bfloat16),
                pltpu.VMEM((swaps, states, channels), jnp.bfloat16),
                pltpu.VMEM((2, rows, cols), jnp.float32),
                pltpu.VMEM((2, rows, cols), jnp.float32),
                pltpu.VMEM((2, rows, cols), jnp.float32),
                pltpu.VMEM((rows, cols), jnp.float32),
                pltpu.VMEM((rows, states, LANES), jnp.float32),
                pltpu.VMEM((rows, states, LANES), jnp.float32),
                pltpu.SemaphoreType.DMA((steps,)),
                pltpu.SemaphoreType.DMA,
                pltpu.SemaphoreType.DMA((parts,)),
                pltpu.SemaphoreType.DMA((parts,)),
                pltpu.SemaphoreType.DMA((parts,)),
                pltpu.SemaphoreType.DMA((swaps,)),
                pltpu.SemaphoreType.DMA((swaps,)),
            ],
            input_output_aliases={given + 11 + k: 2 + k for k in range(3)},
            compiler_params=pltpu.CompilerParams(vmem_limit_bytes=28 * 2**20),
            cost_estimate=pl.CostEstimate(
                flops=4 * rows * channels * (rank + LANES) + 8 * rows * states * channels,
                bytes_accessed=4 * channels * rank + 8 * ROWS * states * channels,
                transcendentals=rows * states * channels,
            ),
            name="step",
        )(
            meta,
            plan,
            *blocks,
            inputs,
            state,
            landed,
            pltpu.with_memory_space_constraint(dt_weight, pltpu.VMEM),
            dt_bias,
            rates,
            skip,
            gain,
            next_gain,
            gate_input,
            pltpu.with_memory_space_constraint(weight, pltpu.VMEM),
            final,
            mixed,
            leaving,
        )

    def send(block, partial):
        axes = ("section", "tensor")
        blocks = []
        for shift in range(peers):
            route = [
                (l * peers + i, (l + 1) % holders * peers + (i + shift) % peers)
                for l in range(holders)
                for i in range(peers)
            ]
            blocks.append(lax.ppermute(partial if shift else block, axes, route))
        return blocks

    def swap(block):
        return lax.all_to_all(block, "section", split_axis=0, concat_axis=0, tiled=True)

    def turn(index, carry):
        blocks, kept = carry
        block, partial, *kept = step(meta_of(index), blocks, *kept)
        return send(block, partial), kept

    picked = pl.pallas_call(
        pick_kernel, out_shape=moved_shape, in_specs=[SMEM, SMEM, VMEM], out_specs=VMEM, name="pick"
    )(place, plan, pool)
    landed = swap(picked)
    *kept, block, partial = empty(
        [state_shape, mixed_shape, moved_shape, block_shape, partial_shape]
    )
    blocks = [block] + [partial] * (peers - 1)
    blocks, kept = lax.fori_loop(-1, turns - 1, turn, (blocks, kept))
    _, _, final, mixed, leaving = step(meta_of(turns - 1), blocks, *kept)
    stored = pl.pallas_call(
        keep_kernel,
        out_shape=jax.ShapeDtypeStruct(pool.shape, pool.dtype),
        in_specs=[SMEM, SMEM, VMEM, VMEM],
        out_specs=VMEM,
        name="keep",
    )(place, plan, pool, swap(leaving))
    return (mixed, final, stored)


def solution(mesh):
    placed = (
        P(None, None, "tensor"),
        P("section", None, None, "tensor"),
        P("section", None, None, "tensor"),
        P("section", "tensor", None),
        P("section", None, "tensor"),
        P("section", "tensor"),
        P("section", None, "tensor"),
        P("section", "tensor"),
        P("section", "tensor"),
        P("section", None, None, "tensor"),
        P(),
        P(),
    )
    return jax.shard_map(
        shards,
        mesh=mesh,
        in_specs=placed,
        out_specs=(
            P("section", None, None, "tensor"),
            P("section", None, None, "tensor"),
            P("section", None, None, "tensor"),
        ),
        check_vma=False,
    )
```

```python
import functools

import jax
import jax.numpy as jnp
from jax import lax
from jax.experimental import pallas as pl
from jax.experimental.pallas import tpu as pltpu
from jax.sharding import PartitionSpec as P

ROWS = 16
LANES = 128
COLS = 1024
DEPTH = 1024
ANY = pl.BlockSpec(memory_space=pl.ANY)
HBM = pl.BlockSpec(memory_space=pltpu.HBM)
VMEM = pl.BlockSpec(memory_space=pltpu.VMEM)
SMEM = pl.BlockSpec(memory_space=pltpu.SMEM)
LOG2E = 1.4426950408889634


def softplus(value):
    small = jnp.exp(-jnp.abs(value))
    return jnp.maximum(value, 0.0) + jnp.where(
        small < 1e-3, small - 0.5 * small * small, jnp.log(1.0 + small)
    )


def finish(total, squares, rank):
    rows, width = total.shape
    extra = width - rank
    lane = lax.broadcasted_iota(jnp.int32, (rows, LANES), 1)
    high = squares.astype(jnp.bfloat16).astype(jnp.float32)
    tail = jnp.concatenate(
        [total[:, rank:], jnp.zeros((rows, LANES - extra), jnp.float32)], axis=1
    )
    tail = jnp.where(lane == extra, high, jnp.where(lane == extra + 1, squares - high, tail))
    return total[:, :rank].astype(jnp.bfloat16), tail.astype(jnp.bfloat16)


def step_kernel(width, layers, peers, *refs):
    meta, plan, arrived = refs[:3]
    others = refs[3 : 2 + peers]
    (
        inputs,
        state,
        landed,
        dt_weight,
        dt_bias,
        rates,
        skip,
        gain,
        next_gain,
        gate,
        next_weight,
        final_in,
        mixed_in,
        leaving_in,
        onward,
        partial,
        final,
        mixed,
        leaving,
        gates,
        result,
        hold,
        held,
        weight,
        coming,
        going,
        size_rows,
        drive_rows,
        base_rows,
        product,
        spread,
        input_sem,
        gate_sem,
        state_sem,
        held_sem,
        weight_sem,
        final_sem,
        mixed_sem,
        coming_sem,
        going_sem,
    ) = refs[2 + peers :]
    steps, rows, channels = gates.shape
    units = steps * rows
    rank = dt_weight.shape[1]
    states = rates.shape[0]
    swaps = going.shape[0]
    cols = min(COLS, channels)
    parts = channels // cols
    depth = min(DEPTH, channels)
    layer = meta[2]
    ahead = (meta[3] == 1) & (layer == layers - 1)
    first = pl.multiple_of(meta[1], ROWS)

    def at(j):
        return pl.ds(pl.multiple_of(j * cols, cols), cols)

    def input_copy(t):
        return pltpu.make_async_copy(
            inputs.at[t, pl.ds(pl.multiple_of(meta[4], ROWS), rows)],
            onward.at[pl.ds(t * rows, rows), pl.ds(0, channels)],
            input_sem.at[t],
        )

    def weight_copy(k):
        span = pl.ds(k * depth, depth)
        return pltpu.make_async_copy(next_weight.at[:, span], weight.at[:, span], weight_sem.at[k])

    def final_copy(j):
        return pltpu.make_async_copy(
            hold.at[:, :, at(j)], final.at[0, pl.ds(first, rows), :, at(j)], final_sem.at[j]
        )

    def mixed_copy(j):
        return pltpu.make_async_copy(
            result.at[:, :, at(j)], mixed.at[0, :, pl.ds(first, rows), at(j)], mixed_sem.at[j]
        )

    @pl.when(ahead)
    def _():
        for t in range(steps):
            input_copy(t).start()

    @pl.when((meta[3] == 1) & (meta[0] == 0))
    def _():
        for k in range(channels // depth):
            weight_copy(k).start()

    @pl.when(meta[0] == 1)
    def _():
        def planned(which, row, k):
            return plan[((which * 3 + row) * layers + layer) * swaps + k]

        gate_copy = pltpu.make_async_copy(gate.at[0, :, pl.ds(first, rows)], gates, gate_sem)

        def held_copy(j):
            return pltpu.make_async_copy(
                dt_weight.at[0, :, at(j)], held.at[:, at(j)], held_sem.at[j]
            )

        def state_copy(j):
            return pltpu.make_async_copy(
                state.at[0, pl.ds(first, rows), :, at(j)], hold.at[:, :, at(j)], state_sem.at[j]
            )

        def coming_copy(k):
            return pltpu.make_async_copy(
                landed.at[planned(0, 1, k)], coming.at[k], coming_sem.at[k]
            )

        def going_copy(k):
            return pltpu.make_async_copy(
                going.at[k], leaving.at[planned(1, 1, k)], going_sem.at[k]
            )

        def inside(which, k):
            place = planned(which, 0, k) - first
            return (place >= 0) & (place < rows)

        gate_copy.start()
        for k in range(swaps):

            @pl.when(inside(0, k))
            def _():
                coming_copy(k).start()

        for j in range(parts):
            held_copy(j).start()
            state_copy(j).start()

        @pl.when(meta[3] == 1)
        def _():
            for k in range(channels // depth):
                weight_copy(k).start()

        total = arrived[:, channels:].astype(jnp.float32)
        for other in others:
            total += other[...].astype(jnp.float32)
        tail = total[:, rank:]
        squares = tail[:, 2 * states : 2 * states + 1] + tail[:, 2 * states + 1 : 2 * states + 2]
        inverse = 1.0 / jnp.sqrt(squares / width + 1e-05)
        low = (total[:, :rank] * inverse).astype(jnp.bfloat16)
        tail = tail * inverse
        turned = tail.T
        for row in range(units):
            column = turned[:states, row : row + 1]
            spread[row] = jnp.broadcast_to(column, (states, LANES)).astype(jnp.bfloat16)
        span = (states, rows * states)
        lane = lax.broadcasted_iota(jnp.int32, span, 1)
        repeat = (lane % states == lax.broadcasted_iota(jnp.int32, span, 0)).astype(jnp.bfloat16)
        span = (rows, rows * states)
        own = lax.broadcasted_iota(jnp.int32, span, 1) // states == lax.broadcasted_iota(
            jnp.int32, span, 0
        )
        outer = tail[:, states : 2 * states].astype(jnp.bfloat16)
        outer = jnp.dot(outer, repeat, preferred_element_type=jnp.float32)
        picks = [
            jnp.where(own, outer[t * rows : (t + 1) * rows], 0.0).astype(jnp.bfloat16)
            for t in range(steps)
        ]
        for k in range(swaps):

            @pl.when(inside(0, k))
            def _():
                coming_copy(k).wait()

        gate_copy.wait()

        def prepare(j, slot):
            here = at(j)
            size = softplus(
                jnp.dot(low, held[:, here], preferred_element_type=jnp.float32) + dt_bias[:, here]
            )
            normed = arrived[:, here].astype(jnp.float32) * gain[:, here] * inverse
            size_rows[slot] = size
            drive_rows[slot] = size * normed
            base_rows[slot] = skip[:, here] * normed

        held_copy(0).wait()
        prepare(0, 0)

        def part(j, carry):
            here = at(j)
            slot = lax.rem(j, 2)
            later = jnp.minimum(j + 1, parts - 1)
            state_copy(j).wait()

            @pl.when(j + 1 < parts)
            def _():
                held_copy(j + 1).wait()


            for k in range(swaps):
                place = planned(0, 0, k) - first

                @pl.when((place >= 0) & (place < rows))
                def _():
                    hold[place, :, here] = coming[k, :, here].astype(jnp.float32)

            rate = rates[:, here]
            for r in range(rows):
                h = hold[r, :, here].astype(jnp.bfloat16)
                for t in range(steps):
                    row = t * rows + r
                    size_row = jnp.broadcast_to(
                        size_rows[slot, row : row + 1, :], (states, cols)
                    ).astype(jnp.bfloat16)
                    drive_row = jnp.broadcast_to(
                        drive_rows[slot, row : row + 1, :], (states, cols)
                    ).astype(jnp.bfloat16)
                    b = jnp.concatenate([spread[row]] * (cols // LANES), axis=1)
                    h = jnp.exp2(size_row * rate) * h + drive_row * b
                    product[t, r * states : (r + 1) * states, :] = h
                hold[r, :, here] = h.astype(jnp.float32)
            summed = jnp.concatenate(
                [
                    jnp.dot(picks[t], product[t], preferred_element_type=jnp.float32)
                    for t in range(steps)
                ],
                axis=0,
            )
            opened = gates[:, :, here].astype(jnp.float32).reshape(units, cols)
            value = (summed + base_rows[slot]) * (opened * jax.nn.sigmoid(opened))
            value = value.astype(jnp.bfloat16)
            result[:, :, here] = value.reshape(steps, rows, cols)
            passed = arrived[:, here].astype(jnp.float32) + value.astype(jnp.float32)
            passed = passed.astype(jnp.bfloat16)
            prepare(later, 1 - slot)

            @pl.when(layer < layers - 1)
            def _():
                onward[:, here] = passed

            final_copy(j).start()
            mixed_copy(j).start()
            return carry

        lax.fori_loop(0, parts, part, 0)
        for k in range(swaps):
            place = planned(1, 0, k) - first

            @pl.when((place >= 0) & (place < rows))
            def _():
                going[k] = hold[place].astype(jnp.bfloat16)
                going_copy(k).start()
                going_copy(k).wait()

    @pl.when(ahead)
    def _():
        for t in range(steps):
            input_copy(t).wait()

    @pl.when(meta[3] == 1)
    def _():
        total = jnp.zeros((units, weight.shape[0]), jnp.float32)
        squares = jnp.zeros((units, 1), jnp.float32)
        for k in range(channels // depth):
            span = pl.ds(k * depth, depth)
            wide = onward[:, span].astype(jnp.float32)
            squares += jnp.sum(wide * wide, axis=1, keepdims=True)
            scaled = (wide * next_gain[:, span]).astype(jnp.bfloat16)
            weight_copy(k).wait()
            total += lax.dot_general(
                scaled,
                weight[:, span],
                (((1,), (1,)), ((), ())),
                preferred_element_type=jnp.float32,
            )
        low, tail = finish(total, squares, rank)
        onward[:, channels : channels + rank] = low
        onward[:, channels + rank :] = tail
        partial[:, :rank] = low
        partial[:, rank:] = tail

    @pl.when(meta[0] == 1)
    def _():
        for j in range(parts):
            mixed_copy(j).wait()
            final_copy(j).wait()


def pick_kernel(meta, plan, store, out):
    layers = out.shape[0]
    swaps = plan.shape[0] // (6 * layers)
    for layer in range(layers):
        slot = 0
        for k in range(swaps):
            asked = plan[(layers + layer) * swaps + k] == meta[0]
            slot = jnp.where(asked, plan[(2 * layers + layer) * swaps + k], slot)
        out[layer] = store[0, slot].astype(out.dtype)


def keep_kernel(meta, plan, store, returned, out):
    layers = returned.shape[0]
    swaps = plan.shape[0] // (6 * layers)
    for slot in range(store.shape[1]):
        source = -1
        for layer in range(layers):
            for k in range(swaps):
                named = (plan[(4 * layers + layer) * swaps + k] == meta[0]) & (
                    plan[(5 * layers + layer) * swaps + k] == slot
                )
                source = jnp.where(named, layer, source)

        @pl.when(source >= 0)
        def _():
            out[0, slot] = returned[source].astype(out.dtype)

        @pl.when(source < 0)
        def _():
            out[0, slot] = store[0, slot]


def leave(*refs):
    pass


def empty(shapes):
    return pl.pallas_call(leave, out_shape=shapes, out_specs=[HBM] * len(shapes))()


def shards(
    inputs,
    state,
    pool,
    x_weight,
    dt_weight,
    dt_bias,
    a_log,
    skip,
    gain,
    gate_input,
    swap_plan,
    evict_plan,
):
    section = lax.axis_index("section")
    holders = lax.axis_size("section")
    peers = lax.axis_size("tensor")
    channels = x_weight.shape[1]
    width = channels * peers
    rank = dt_weight.shape[1]
    states = a_log.shape[1]
    requests = state.shape[1]
    steps = inputs.shape[0]
    swaps = swap_plan.shape[2]
    units = requests // ROWS
    rows = steps * ROWS
    cols = min(COLS, channels)
    parts = channels // cols
    depth = min(DEPTH, channels)
    turns = units + holders - 1
    plan = jnp.concatenate([swap_plan.reshape(-1), evict_plan.reshape(-1)])
    down = [((i + 1) % holders, i) for i in range(holders)]
    weight = lax.ppermute(jnp.swapaxes(x_weight[0], 0, 1), "section", down)
    next_gain = lax.ppermute(gain, "section", down)
    rates = (-LOG2E * jnp.exp(a_log[0])).astype(jnp.bfloat16)
    place = section.astype(jnp.int32)[None]

    block_shape = jax.ShapeDtypeStruct((rows, channels + rank + LANES), jnp.bfloat16)
    partial_shape = jax.ShapeDtypeStruct((rows, rank + LANES), jnp.bfloat16)
    stream_shape = (steps, ROWS, channels)
    state_shape = jax.ShapeDtypeStruct(state.shape, state.dtype)
    mixed_shape = jax.ShapeDtypeStruct(gate_input.shape, gate_input.dtype)
    moved_shape = jax.ShapeDtypeStruct((holders, states, channels), jnp.bfloat16)

    def meta_of(turn):
        unit = turn - section
        valid = (unit >= 0) & (unit < units)
        last = section == holders - 1
        following = turn + 1
        ahead = jnp.where(last, following < units, valid)
        first = jnp.clip(unit, 0, units - 1) * ROWS
        then = jnp.clip(following, 0, units - 1) * ROWS
        return jnp.stack([valid, first, section, ahead, then]).astype(jnp.int32)

    def step(meta, blocks, final, mixed, leaving):
        given = 2 + peers
        return pl.pallas_call(
            functools.partial(step_kernel, width, holders, peers),
            out_shape=[block_shape, partial_shape, state_shape, mixed_shape, moved_shape],
            in_specs=[SMEM, SMEM]
            + [VMEM] * peers
            + [HBM, HBM, ANY, HBM]
            + [VMEM] * 5
            + [HBM, HBM]
            + [HBM] * 3,
            out_specs=[VMEM, VMEM, HBM, HBM, HBM],
            scratch_shapes=[
                pltpu.VMEM(stream_shape, jnp.bfloat16),
                pltpu.VMEM(stream_shape, jnp.bfloat16),
                pltpu.VMEM((ROWS, states, channels), jnp.float32),
                pltpu.VMEM((rank, channels), jnp.bfloat16),
                pltpu.VMEM(weight.shape, jnp.bfloat16),
                pltpu.VMEM((swaps, states, channels), jnp.bfloat16),
                pltpu.VMEM((swaps, states, channels), jnp.bfloat16),
                pltpu.VMEM((2, rows, cols), jnp.float32),
                pltpu.VMEM((2, rows, cols), jnp.float32),
                pltpu.VMEM((2, rows, cols), jnp.float32),
                pltpu.VMEM((steps, ROWS * states, cols), jnp.bfloat16),
                pltpu.VMEM((rows, states, LANES), jnp.bfloat16),
                pltpu.SemaphoreType.DMA((steps,)),
                pltpu.SemaphoreType.DMA,
                pltpu.SemaphoreType.DMA((parts,)),
                pltpu.SemaphoreType.DMA((parts,)),
                pltpu.SemaphoreType.DMA((channels // depth,)),
                pltpu.SemaphoreType.DMA((parts,)),
                pltpu.SemaphoreType.DMA((parts,)),
                pltpu.SemaphoreType.DMA((swaps,)),
                pltpu.SemaphoreType.DMA((swaps,)),
            ],
            input_output_aliases={given + 11 + k: 2 + k for k in range(3)},
            compiler_params=pltpu.CompilerParams(vmem_limit_bytes=24 * 2**20),
            cost_estimate=pl.CostEstimate(
                flops=4 * rows * channels * (rank + LANES) + 8 * rows * states * channels,
                bytes_accessed=4 * channels * rank + 8 * ROWS * states * channels,
                transcendentals=rows * states * channels,
            ),
            name="step",
        )(
            meta,
            plan,
            *blocks,
            inputs,
            state,
            landed,
            dt_weight,
            dt_bias,
            rates,
            skip,
            gain,
            next_gain,
            gate_input,
            weight,
            final,
            mixed,
            leaving,
        )

    def send(block, partial):
        axes = ("section", "tensor")
        blocks = []
        for shift in range(peers):
            route = [
                (l * peers + i, (l + 1) % holders * peers + (i + shift) % peers)
                for l in range(holders)
                for i in range(peers)
            ]
            blocks.append(lax.ppermute(partial if shift else block, axes, route))
        return blocks

    def swap(block):
        return lax.all_to_all(block, "section", split_axis=0, concat_axis=0, tiled=True)

    def turn(index, carry):
        blocks, kept = carry
        block, partial, *kept = step(meta_of(index), blocks, *kept)
        return send(block, partial), kept

    picked = pl.pallas_call(
        pick_kernel, out_shape=moved_shape, in_specs=[SMEM, SMEM, VMEM], out_specs=VMEM, name="pick"
    )(place, plan, pool)
    landed = swap(picked)
    *kept, block, partial = empty(
        [state_shape, mixed_shape, moved_shape, block_shape, partial_shape]
    )
    blocks = [block] + [partial] * (peers - 1)
    blocks, kept = lax.fori_loop(-1, turns - 1, turn, (blocks, kept))
    _, _, final, mixed, leaving = step(meta_of(turns - 1), blocks, *kept)
    stored = pl.pallas_call(
        keep_kernel,
        out_shape=jax.ShapeDtypeStruct(pool.shape, pool.dtype),
        in_specs=[SMEM, SMEM, VMEM, VMEM],
        out_specs=VMEM,
        name="keep",
    )(place, plan, pool, swap(leaving))
    return (mixed, final, stored)


def solution(mesh):
    placed = (
        P(None, None, "tensor"),
        P("section", None, None, "tensor"),
        P("section", None, None, "tensor"),
        P("section", "tensor", None),
        P("section", None, "tensor"),
        P("section", "tensor"),
        P("section", None, "tensor"),
        P("section", "tensor"),
        P("section", "tensor"),
        P("section", None, None, "tensor"),
        P(),
        P(),
    )
    return jax.shard_map(
        shards,
        mesh=mesh,
        in_specs=placed,
        out_specs=(
            P("section", None, None, "tensor"),
            P("section", None, None, "tensor"),
            P("section", None, None, "tensor"),
        ),
        check_vma=False,
    )
```

```python
import functools

import jax
import jax.numpy as jnp
from jax import lax
from jax.experimental import pallas as pl
from jax.experimental.pallas import tpu as pltpu
from jax.sharding import PartitionSpec as P

ROWS = 16
LANES = 128
COLS = 512
DEPTH = 1024
ANY = pl.BlockSpec(memory_space=pl.ANY)
HBM = pl.BlockSpec(memory_space=pltpu.HBM)
VMEM = pl.BlockSpec(memory_space=pltpu.VMEM)
SMEM = pl.BlockSpec(memory_space=pltpu.SMEM)
LOG2E = 1.4426950408889634


def softplus(value):
    small = jnp.exp(-jnp.abs(value))
    return jnp.maximum(value, 0.0) + jnp.where(
        small < 1e-3, small - 0.5 * small * small, jnp.log(1.0 + small)
    )


def finish(total, squares, rank):
    rows, width = total.shape
    extra = width - rank
    lane = lax.broadcasted_iota(jnp.int32, (rows, LANES), 1)
    high = squares.astype(jnp.bfloat16).astype(jnp.float32)
    tail = jnp.concatenate(
        [total[:, rank:], jnp.zeros((rows, LANES - extra), jnp.float32)], axis=1
    )
    tail = jnp.where(lane == extra, high, jnp.where(lane == extra + 1, squares - high, tail))
    return total[:, :rank].astype(jnp.bfloat16), tail.astype(jnp.bfloat16)


def project(onward, partial, gain, weight, copy):
    units = onward.shape[0]
    rank = partial.shape[1] - LANES
    channels = weight.shape[1]
    depth = min(DEPTH, channels)
    total = jnp.zeros((units, weight.shape[0]), jnp.float32)
    squares = jnp.zeros((units, 1), jnp.float32)
    for k in range(channels // depth):
        span = pl.ds(k * depth, depth)
        wide = onward[:, span].astype(jnp.float32)
        squares += jnp.sum(wide * wide, axis=1, keepdims=True)
        scaled = (wide * gain[:, span]).astype(jnp.bfloat16)
        copy(k).wait()
        total += lax.dot_general(
            scaled,
            weight[:, span],
            (((1,), (1,)), ((), ())),
            preferred_element_type=jnp.float32,
        )
    low, tail = finish(total, squares, rank)
    onward[:, channels : channels + rank] = low
    onward[:, channels + rank :] = tail
    partial[:, :rank] = low
    partial[:, rank:] = tail


def open_kernel(place, inputs, gain, own_weight, onward, partial, weight, input_sem, weight_sem):
    steps = inputs.shape[0]
    channels = weight.shape[1]
    depth = min(DEPTH, channels)

    def weight_copy(k):
        span = pl.ds(k * depth, depth)
        return pltpu.make_async_copy(own_weight.at[:, span], weight.at[:, span], weight_sem.at[k])

    def input_copy(t):
        return pltpu.make_async_copy(
            inputs.at[t, pl.ds(0, ROWS)],
            onward.at[pl.ds(t * ROWS, ROWS), pl.ds(0, channels)],
            input_sem.at[t],
        )

    @pl.when(place[0] == 0)
    def _():
        for t in range(steps):
            input_copy(t).start()
        for k in range(channels // depth):
            weight_copy(k).start()
        for t in range(steps):
            input_copy(t).wait()
        project(onward, partial, gain, weight, weight_copy)


def step_kernel(width, layers, peers, *refs):
    meta, plan, arrived = refs[:3]
    others = refs[3 : 2 + peers]
    (
        inputs,
        state,
        landed,
        dt_weight,
        dt_bias,
        rates,
        skip,
        gain,
        next_gain,
        gate,
        next_weight,
        final_in,
        mixed_in,
        leaving_in,
        onward,
        partial,
        final,
        mixed,
        leaving,
        gates,
        result,
        hold,
        held,
        weight,
        coming,
        going,
        size_rows,
        drive_rows,
        base_rows,
        product,
        spread,
        input_sem,
        gate_sem,
        state_sem,
        held_sem,
        weight_sem,
        final_sem,
        mixed_sem,
        coming_sem,
        going_sem,
    ) = refs[2 + peers :]
    steps, rows, channels = gates.shape
    units = steps * rows
    rank = dt_weight.shape[1]
    states = rates.shape[0]
    swaps = going.shape[0]
    cols = min(COLS, channels)
    parts = channels // cols
    depth = min(DEPTH, channels)
    layer = meta[2]
    ahead = (meta[3] == 1) & (layer == layers - 1)
    first = pl.multiple_of(meta[1], ROWS)

    def at(j):
        return pl.ds(pl.multiple_of(j * cols, cols), cols)

    def input_copy(t):
        return pltpu.make_async_copy(
            inputs.at[t, pl.ds(pl.multiple_of(meta[4], ROWS), rows)],
            onward.at[pl.ds(t * rows, rows), pl.ds(0, channels)],
            input_sem.at[t],
        )

    def weight_copy(k):
        span = pl.ds(k * depth, depth)
        return pltpu.make_async_copy(next_weight.at[:, span], weight.at[:, span], weight_sem.at[k])

    def final_copy(j):
        return pltpu.make_async_copy(
            hold.at[:, :, at(j)], final.at[0, pl.ds(first, rows), :, at(j)], final_sem.at[j]
        )

    def mixed_copy(j):
        return pltpu.make_async_copy(
            result.at[:, :, at(j)], mixed.at[0, :, pl.ds(first, rows), at(j)], mixed_sem.at[j]
        )

    @pl.when(ahead)
    def _():
        for t in range(steps):
            input_copy(t).start()

    @pl.when((meta[3] == 1) & (meta[0] == 0))
    def _():
        for k in range(channels // depth):
            weight_copy(k).start()

    @pl.when(meta[0] == 1)
    def _():
        def planned(which, row, k):
            return plan[((which * 3 + row) * layers + layer) * swaps + k]

        gate_copy = pltpu.make_async_copy(gate.at[0, :, pl.ds(first, rows)], gates, gate_sem)

        def held_copy(j):
            return pltpu.make_async_copy(
                dt_weight.at[0, :, at(j)], held.at[:, at(j)], held_sem.at[j]
            )

        def state_copy(j):
            return pltpu.make_async_copy(
                state.at[0, pl.ds(first, rows), :, at(j)], hold.at[:, :, at(j)], state_sem.at[j]
            )

        def coming_copy(k):
            return pltpu.make_async_copy(
                landed.at[planned(0, 1, k)], coming.at[k], coming_sem.at[k]
            )

        def going_copy(k):
            return pltpu.make_async_copy(
                going.at[k], leaving.at[planned(1, 1, k)], going_sem.at[k]
            )

        def inside(which, k):
            place = planned(which, 0, k) - first
            return (place >= 0) & (place < rows)

        gate_copy.start()
        for k in range(swaps):

            @pl.when(inside(0, k))
            def _():
                coming_copy(k).start()

        for j in range(parts):
            held_copy(j).start()
            state_copy(j).start()

        @pl.when(meta[3] == 1)
        def _():
            for k in range(channels // depth):
                weight_copy(k).start()

        total = arrived[:, channels:].astype(jnp.float32)
        for other in others:
            total += other[...].astype(jnp.float32)
        tail = total[:, rank:]
        squares = tail[:, 2 * states : 2 * states + 1] + tail[:, 2 * states + 1 : 2 * states + 2]
        inverse = 1.0 / jnp.sqrt(squares / width + 1e-05)
        low = (total[:, :rank] * inverse).astype(jnp.bfloat16)
        tail = tail * inverse
        turned = tail.T
        for row in range(units):
            column = turned[:states, row : row + 1]
            spread[row] = jnp.broadcast_to(column, (states, LANES)).astype(jnp.bfloat16)
        span = (states, rows * states)
        lane = lax.broadcasted_iota(jnp.int32, span, 1)
        repeat = (lane % states == lax.broadcasted_iota(jnp.int32, span, 0)).astype(jnp.bfloat16)
        span = (rows, rows * states)
        own = lax.broadcasted_iota(jnp.int32, span, 1) // states == lax.broadcasted_iota(
            jnp.int32, span, 0
        )
        outer = tail[:, states : 2 * states].astype(jnp.bfloat16)
        outer = jnp.dot(outer, repeat, preferred_element_type=jnp.float32)
        picks = [
            jnp.where(own, outer[t * rows : (t + 1) * rows], 0.0).astype(jnp.bfloat16)
            for t in range(steps)
        ]
        for k in range(swaps):

            @pl.when(inside(0, k))
            def _():
                coming_copy(k).wait()

        gate_copy.wait()

        def prepare(j, slot):
            here = at(j)
            size = softplus(
                jnp.dot(low, held[:, here], preferred_element_type=jnp.float32) + dt_bias[:, here]
            )
            normed = arrived[:, here].astype(jnp.float32) * gain[:, here] * inverse
            size_rows[slot] = size
            drive_rows[slot] = size * normed
            base_rows[slot] = skip[:, here] * normed

        held_copy(0).wait()
        prepare(0, 0)

        def part(j, carry):
            here = at(j)
            slot = lax.rem(j, 2)
            later = jnp.minimum(j + 1, parts - 1)
            state_copy(j).wait()

            @pl.when(j + 1 < parts)
            def _():
                held_copy(j + 1).wait()


            for k in range(swaps):
                place = planned(0, 0, k) - first

                @pl.when((place >= 0) & (place < rows))
                def _():
                    hold[place, :, here] = coming[k, :, here].astype(jnp.float32)

            rate = rates[:, here]
            for r in range(rows):
                h = hold[r, :, here].astype(jnp.bfloat16)
                for t in range(steps):
                    row = t * rows + r
                    size_row = jnp.broadcast_to(
                        size_rows[slot, row : row + 1, :], (states, cols)
                    ).astype(jnp.bfloat16)
                    drive_row = jnp.broadcast_to(
                        drive_rows[slot, row : row + 1, :], (states, cols)
                    ).astype(jnp.bfloat16)
                    b = jnp.concatenate([spread[row]] * (cols // LANES), axis=1)
                    h = jnp.exp2(size_row * rate) * h + drive_row * b
                    product[t, r * states : (r + 1) * states, :] = h
                hold[r, :, here] = h.astype(jnp.float32)
            summed = jnp.concatenate(
                [
                    jnp.dot(picks[t], product[t], preferred_element_type=jnp.float32)
                    for t in range(steps)
                ],
                axis=0,
            )
            opened = gates[:, :, here].astype(jnp.float32).reshape(units, cols)
            value = (summed + base_rows[slot]) * (opened * jax.nn.sigmoid(opened))
            value = value.astype(jnp.bfloat16)
            result[:, :, here] = value.reshape(steps, rows, cols)
            passed = arrived[:, here].astype(jnp.float32) + value.astype(jnp.float32)
            passed = passed.astype(jnp.bfloat16)
            prepare(later, 1 - slot)

            @pl.when(layer < layers - 1)
            def _():
                onward[:, here] = passed

            final_copy(j).start()
            mixed_copy(j).start()
            return carry

        lax.fori_loop(0, parts, part, 0)
        for k in range(swaps):
            place = planned(1, 0, k) - first

            @pl.when((place >= 0) & (place < rows))
            def _():
                going[k] = hold[place].astype(jnp.bfloat16)
                going_copy(k).start()
                going_copy(k).wait()

    @pl.when(ahead)
    def _():
        for t in range(steps):
            input_copy(t).wait()

    @pl.when(meta[3] == 1)
    def _():
        project(onward, partial, next_gain, weight, weight_copy)

    @pl.when(meta[0] == 1)
    def _():
        for j in range(parts):
            mixed_copy(j).wait()
            final_copy(j).wait()


def pick_kernel(meta, plan, store, out):
    layers = out.shape[0]
    swaps = plan.shape[0] // (6 * layers)
    for layer in range(layers):
        slot = 0
        for k in range(swaps):
            asked = plan[(layers + layer) * swaps + k] == meta[0]
            slot = jnp.where(asked, plan[(2 * layers + layer) * swaps + k], slot)
        out[layer] = store[0, slot].astype(out.dtype)


def keep_kernel(meta, plan, store, returned, out):
    layers = returned.shape[0]
    swaps = plan.shape[0] // (6 * layers)
    for slot in range(store.shape[1]):
        source = -1
        for layer in range(layers):
            for k in range(swaps):
                named = (plan[(4 * layers + layer) * swaps + k] == meta[0]) & (
                    plan[(5 * layers + layer) * swaps + k] == slot
                )
                source = jnp.where(named, layer, source)

        @pl.when(source >= 0)
        def _():
            out[0, slot] = returned[source].astype(out.dtype)

        @pl.when(source < 0)
        def _():
            out[0, slot] = store[0, slot]


def leave(*refs):
    pass


def empty(shapes):
    return pl.pallas_call(leave, out_shape=shapes, out_specs=[HBM] * len(shapes))()


def shards(
    inputs,
    state,
    pool,
    x_weight,
    dt_weight,
    dt_bias,
    a_log,
    skip,
    gain,
    gate_input,
    swap_plan,
    evict_plan,
):
    section = lax.axis_index("section")
    holders = lax.axis_size("section")
    peers = lax.axis_size("tensor")
    channels = x_weight.shape[1]
    width = channels * peers
    rank = dt_weight.shape[1]
    states = a_log.shape[1]
    requests = state.shape[1]
    steps = inputs.shape[0]
    swaps = swap_plan.shape[2]
    units = requests // ROWS
    rows = steps * ROWS
    cols = min(COLS, channels)
    parts = channels // cols
    depth = min(DEPTH, channels)
    turns = units + holders - 1
    plan = jnp.concatenate([swap_plan.reshape(-1), evict_plan.reshape(-1)])
    down = [((i + 1) % holders, i) for i in range(holders)]
    own_weight = jnp.swapaxes(x_weight[0], 0, 1)
    weight = lax.ppermute(own_weight, "section", down)
    next_gain = lax.ppermute(gain, "section", down)
    rates = (-LOG2E * jnp.exp(a_log[0])).astype(jnp.bfloat16)
    place = section.astype(jnp.int32)[None]

    block_shape = jax.ShapeDtypeStruct((rows, channels + rank + LANES), jnp.bfloat16)
    partial_shape = jax.ShapeDtypeStruct((rows, rank + LANES), jnp.bfloat16)
    stream_shape = (steps, ROWS, channels)
    state_shape = jax.ShapeDtypeStruct(state.shape, state.dtype)
    mixed_shape = jax.ShapeDtypeStruct(gate_input.shape, gate_input.dtype)
    moved_shape = jax.ShapeDtypeStruct((holders, states, channels), jnp.bfloat16)

    def meta_of(turn):
        unit = turn - section
        valid = (unit >= 0) & (unit < units)
        last = section == holders - 1
        following = turn + 1
        ahead = jnp.where(last, following < units, valid)
        first = jnp.clip(unit, 0, units - 1) * ROWS
        then = jnp.clip(following, 0, units - 1) * ROWS
        return jnp.stack([valid, first, section, ahead, then]).astype(jnp.int32)

    def step(meta, blocks, final, mixed, leaving):
        given = 2 + peers
        return pl.pallas_call(
            functools.partial(step_kernel, width, holders, peers),
            out_shape=[block_shape, partial_shape, state_shape, mixed_shape, moved_shape],
            in_specs=[SMEM, SMEM]
            + [VMEM] * peers
            + [HBM, HBM, ANY, HBM]
            + [VMEM] * 5
            + [HBM, HBM]
            + [HBM] * 3,
            out_specs=[VMEM, VMEM, HBM, HBM, HBM],
            scratch_shapes=[
                pltpu.VMEM(stream_shape, jnp.bfloat16),
                pltpu.VMEM(stream_shape, jnp.bfloat16),
                pltpu.VMEM((ROWS, states, channels), jnp.float32),
                pltpu.VMEM((rank, channels), jnp.bfloat16),
                pltpu.VMEM(weight.shape, jnp.bfloat16),
                pltpu.VMEM((swaps, states, channels), jnp.bfloat16),
                pltpu.VMEM((swaps, states, channels), jnp.bfloat16),
                pltpu.VMEM((2, rows, cols), jnp.float32),
                pltpu.VMEM((2, rows, cols), jnp.float32),
                pltpu.VMEM((2, rows, cols), jnp.float32),
                pltpu.VMEM((steps, ROWS * states, cols), jnp.bfloat16),
                pltpu.VMEM((rows, states, LANES), jnp.bfloat16),
                pltpu.SemaphoreType.DMA((steps,)),
                pltpu.SemaphoreType.DMA,
                pltpu.SemaphoreType.DMA((parts,)),
                pltpu.SemaphoreType.DMA((parts,)),
                pltpu.SemaphoreType.DMA((channels // depth,)),
                pltpu.SemaphoreType.DMA((parts,)),
                pltpu.SemaphoreType.DMA((parts,)),
                pltpu.SemaphoreType.DMA((swaps,)),
                pltpu.SemaphoreType.DMA((swaps,)),
            ],
            input_output_aliases={given + 11 + k: 2 + k for k in range(3)},
            compiler_params=pltpu.CompilerParams(vmem_limit_bytes=24 * 2**20),
            cost_estimate=pl.CostEstimate(
                flops=4 * rows * channels * (rank + LANES) + 8 * rows * states * channels,
                bytes_accessed=4 * channels * rank + 8 * ROWS * states * channels,
                transcendentals=rows * states * channels,
            ),
            name="step",
        )(
            meta,
            plan,
            *blocks,
            inputs,
            state,
            landed,
            dt_weight,
            dt_bias,
            rates,
            skip,
            gain,
            next_gain,
            gate_input,
            weight,
            final,
            mixed,
            leaving,
        )

    def send(block, partial):
        axes = ("section", "tensor")
        blocks = []
        for shift in range(peers):
            route = [
                (l * peers + i, (l + 1) % holders * peers + (i + shift) % peers)
                for l in range(holders)
                for i in range(peers)
            ]
            blocks.append(lax.ppermute(partial if shift else block, axes, route))
        return blocks

    def swap(block):
        return lax.all_to_all(block, "section", split_axis=0, concat_axis=0, tiled=True)

    def turn(index, carry):
        blocks, kept = carry
        block, partial, *kept = step(meta_of(index), blocks, *kept)
        return send(block, partial), kept

    picked = pl.pallas_call(
        pick_kernel, out_shape=moved_shape, in_specs=[SMEM, SMEM, VMEM], out_specs=VMEM, name="pick"
    )(place, plan, pool)
    landed = swap(picked)
    block, partial = pl.pallas_call(
        open_kernel,
        out_shape=[block_shape, partial_shape],
        in_specs=[SMEM, HBM, VMEM, HBM],
        out_specs=[VMEM, VMEM],
        scratch_shapes=[
            pltpu.VMEM(weight.shape, jnp.bfloat16),
            pltpu.SemaphoreType.DMA((steps,)),
            pltpu.SemaphoreType.DMA((channels // depth,)),
        ],
        compiler_params=pltpu.CompilerParams(vmem_limit_bytes=24 * 2**20),
        name="open",
    )(place, inputs, gain, own_weight)
    blocks = [block]
    for shift in range(1, peers):
        route = [(i, (i + shift) % peers) for i in range(peers)]
        blocks.append(lax.ppermute(partial, "tensor", route))
    kept = list(empty([state_shape, mixed_shape, moved_shape]))
    blocks, kept = lax.fori_loop(0, turns - 1, turn, (blocks, kept))
    _, _, final, mixed, leaving = step(meta_of(turns - 1), blocks, *kept)
    stored = pl.pallas_call(
        keep_kernel,
        out_shape=jax.ShapeDtypeStruct(pool.shape, pool.dtype),
        in_specs=[SMEM, SMEM, VMEM, VMEM],
        out_specs=VMEM,
        name="keep",
    )(place, plan, pool, swap(leaving))
    return (mixed, final, stored)


def solution(mesh):
    placed = (
        P(None, None, "tensor"),
        P("section", None, None, "tensor"),
        P("section", None, None, "tensor"),
        P("section", "tensor", None),
        P("section", None, "tensor"),
        P("section", "tensor"),
        P("section", None, "tensor"),
        P("section", "tensor"),
        P("section", "tensor"),
        P("section", None, None, "tensor"),
        P(),
        P(),
    )
    return jax.shard_map(
        shards,
        mesh=mesh,
        in_specs=placed,
        out_specs=(
            P("section", None, None, "tensor"),
            P("section", None, None, "tensor"),
            P("section", None, None, "tensor"),
        ),
        check_vma=False,
    )
```
